32 devices in a mesh: dp: 2 (over x), expert: 16 (over z, y, core).
Axes of the slice: x: 2, y: 2, z: 4, core: 2. Of those that a mesh axis runs over, the one named last changes fastest.
Arguments:
- tokens: bfloat16 [4096, 2048], P(('dp', 'expert')), may hold values from -6 to 6
- out_grad: bfloat16 [4096, 2048], P(('dp', 'expert')), may hold values from -6 to 6
- expert_ids: int32 [4096, 6], P(('dp', 'expert')), may hold values from 0 to 15, all different within a row; in each aligned block of 128 rows (0 to 127, 128 to 255, ...) at most 49 rows name the same one
- gate_weights: float32 [4096, 6], P(('dp', 'expert')), may hold values from 0.05 to 1
- trained: int32 [4], replicated, may hold values from 0 to 15, as said below
- w_in: bfloat16 [16, 2048, 1408], P('expert'), may hold values from -0.125 to 0.125
- w_down: bfloat16 [16, 704, 2048], P('expert'), may hold values from -0.21875 to 0.21875
- saved: bfloat16 [2, 16, 784, 1408], P('dp', 'expert'), may hold values from -6 to 6
Outputs:
- in_grad: bfloat16 [4096, 2048], P(('dp', 'expert'))
- weight_grad: bfloat16 [16, 2048, 2112], P('expert', 'dp')
The draws below stay inside these ranges and needn't reach their ends.
Inputs may be any that keep to these rules, and one draw needn't show every extreme that they name: `expert_ids`: among the 128 tokens of one device no expert is named more than 49 times, a bound that some block reaches; a token names 6 different experts. `trained`: 4 different expert ids; the ids 0 and 15 are always among them.
All inputs are finite; a program needn't handle non-finite values.
Results may differ from the reference program's by a relative error of at most 0.017.
Values may be sent and summed in bfloat16 or wider, within the bound.
No kernel may reach another device: no remote copies, remote signals or barrier semaphores. Data moves between devices by JAX's collectives and lax.ppermute only.
A program may use at most 128 MiB of HBM per device.

```python
import math
import jax
import jax.numpy as jnp
import numpy as np
from jax import lax

D = 2048
FF = 704
TOP = 6
TOK_DEV = 128
EXPERTS = 16
CAP = 49
N_TRAIN = 4
TOKENS = 4096
N_DP = 2
N_EXPERT = 16
DEVICES = 32


def draw_trained(key, part):
    inner_key = jax.random.fold_in(key, 11)
    order_key = jax.random.fold_in(key, 23)
    middle = jax.random.permutation(inner_key, EXPERTS - 2)[:N_TRAIN - 2].astype(jnp.int32) + 1
    ends = jnp.array([0, EXPERTS - 1], dtype=jnp.int32)
    chosen = jnp.concatenate([ends, middle]).astype(jnp.int32)
    return jax.random.permutation(order_key, chosen).astype(jnp.int32)


def shard_levels(rng, shape, shards, least, high):
    factor_of, own = 1.0, jax.random.fold_in(rng, 6)
    for dim, parts in shards:
        steps = jnp.exp(jax.random.uniform(jax.random.fold_in(own, dim), (parts,), jnp.float32, least / len(shards), high / len(shards)))
        factor_of = factor_of * jnp.repeat(steps, shape[dim] // parts).reshape([-1 if axis == dim else 1 for axis in range(len(shape))])
    return factor_of


def deal_out(key, own, number, rows, amount, top, limit, lean):
    order = jax.random.permutation(key, amount)
    packed, common = portions_of(amount, rows * top, limit, lean, True), portions_of(amount, rows * top, limit, lean, False)
    places = jnp.arange(amount)

    def named(lengths, rotation):
        used = int((lengths > 0).sum())
        fixed = max(1, used // 4)
        moved = fixed + (places - fixed + rotation * (used - fixed)) % max(1, amount - fixed)
        return jnp.zeros((amount,), jnp.int32).at[order[jnp.where(places < fixed, places, moved)]].set(jnp.asarray(lengths, jnp.int32))

    lengths = jnp.where(number % 4 == 0, named(packed, number // 4), named(common, number - number // 4 - 1))
    mixed = jax.random.permutation(jax.random.fold_in(own, 3), amount)
    donor, sink = mixed[0:amount // 2 * 2:2], mixed[1:amount // 2 * 2:2]
    margin = jnp.minimum(lengths[donor] - 1, limit - lengths[sink]) // 2
    margin = jnp.where((donor == order[0]) | (sink == order[0]) | (lengths[sink] == 0), 0, jnp.maximum(margin, 0))
    moved = jax.random.randint(jax.random.fold_in(own, 4), (amount // 2,), 0, 1 << 20) % (margin + 1)
    lengths = lengths.at[donor].add(-moved).at[sink].add(moved)
    items = jnp.searchsorted(jnp.cumsum(lengths), jnp.arange(rows * top), side="right").astype(jnp.int32)
    listing = items.reshape(top, rows).T
    listing = listing[jax.random.permutation(jax.random.fold_in(own, 1), rows)]
    rotation = jax.random.randint(jax.random.fold_in(own, 2), (rows, 1), 0, top)
    return jnp.take_along_axis(listing, (jnp.arange(top)[None, :] + rotation) % top, axis=1)


def portions_of(amount, total, most, slope, full):
    portions = [(1 << 20) // math.isqrt(grade ** slope) + 1 for grade in range(1, amount + 1)]
    largest = most if full else min(most, max(-(-total // amount), total * portions[0] // sum(portions)))
    least = 1 if total - largest >= amount - 1 else 0
    given, rest = [largest] + [least] * (amount - 1), total - largest - least * (amount - 1)
    while rest > 0:
        candidates = [i for i in range(1, amount) if given[i] < largest] or [i for i in range(1, amount) if given[i] < most]
        whole, budget = sum([portions[i] for i in candidates]), rest
        for i in candidates:
            more = min(most - given[i], max(1, budget * portions[i] // whole), rest)
            given[i] = given[i] + more
            rest = rest - more
    return np.array(given)


def gaussian(own_key, shape, spread, bound, pieces=(), held_as=jnp.bfloat16):
    values = jax.random.normal(own_key, shape, jnp.float32) * spread
    if len(pieces) > 0:
        values = shard_levels(own_key, shape, pieces, -0.22, 0.18) * values
    return jnp.clip(values, min=-bound, max=bound).astype(held_as)


def setup_inputs(seed: int = 0) -> dict:
    keys = jax.random.split(jax.random.key(seed), 9)
    tokens = gaussian(keys[0], (TOKENS, D), 1.0, 6.0, ((0, 32),))
    out_grad = gaussian(keys[1], (TOKENS, D), 1.0, 6.0, ((0, 32),))
    expert_ids_keys = jax.random.split(jax.random.fold_in(keys[2], 1), TOKENS // TOK_DEV)
    expert_ids_turns = jax.random.permutation(jax.random.fold_in(keys[2], 3), TOKENS // TOK_DEV)
    expert_ids = jax.vmap(lambda own, number: deal_out(jax.random.fold_in(keys[2], 2), own, number, TOK_DEV, EXPERTS, TOP, CAP, 2))(expert_ids_keys, expert_ids_turns).reshape((TOKENS, TOP))
    gate_weights = jnp.clip(jnp.exp(math.log(1.0) - 2.9957323 * jax.random.uniform(keys[3], (TOKENS, TOP), jnp.float32) ** shard_levels(keys[3], (TOKENS, TOP), ((0, 32),), -0.2, 0.2)), 0.05, 1.0)
    trained = draw_trained(jax.random.fold_in(keys[8], 71), 0)
    w_in = gaussian(keys[5], (EXPERTS, D, 2 * FF), D ** -0.5, 0.125, ((0, 16),))
    w_down = gaussian(keys[6], (EXPERTS, FF, D), FF ** -0.5, 0.21875, ((0, 16),))
    saved = gaussian(keys[7], (N_DP, EXPERTS, N_EXPERT * CAP, 2 * FF), 1.0, 6.0, ((0, 2), (1, 16)))
    return dict(tokens=tokens, out_grad=out_grad, expert_ids=expert_ids, gate_weights=gate_weights, trained=trained, w_in=w_in, w_down=w_down, saved=saved)


def reference(tokens, out_grad, expert_ids, gate_weights, trained, w_in, w_down, saved):
    entry_count = TOK_DEV * TOP
    flat_ids = expert_ids.reshape(DEVICES, entry_count).astype(jnp.int32)
    labels = jnp.arange(EXPERTS, dtype=jnp.int32)
    onehot = (flat_ids[:, :, None] == labels[None, None, :]).astype(jnp.int32)
    slot_rank = jnp.sum(jnp.cumsum(onehot, axis=1) * onehot, axis=2) - 1
    slot_index = (flat_ids * CAP + slot_rank).astype(jnp.int32)
    device_rows = jnp.broadcast_to(jnp.arange(DEVICES, dtype=jnp.int32)[:, None], (DEVICES, entry_count))
    entries = (device_rows * entry_count + jnp.arange(entry_count, dtype=jnp.int32)[None, :]).astype(jnp.int32)
    source = jnp.zeros((DEVICES, EXPERTS * CAP), jnp.int32).at[device_rows, slot_index].set(entries)
    filled = jnp.zeros((DEVICES, EXPERTS * CAP), jnp.float32).at[device_rows, slot_index].set(1.0)
    gate_flat = gate_weights.reshape(-1)

    def one_expert(in_accum, expert):
        start = (expert * CAP).astype(jnp.int32)
        entry_list = lax.dynamic_slice_in_dim(source, start, CAP, 1).reshape(-1)
        live_mask = lax.dynamic_slice_in_dim(filled, start, CAP, 1).reshape(-1)[:, None]
        tok_index = (entry_list // TOP).astype(jnp.int32)
        tok_rows = (tokens[tok_index].astype(jnp.float32) * live_mask).astype(jnp.bfloat16)
        scaled = (gate_flat[entry_list][:, None] * out_grad[tok_index].astype(jnp.float32) * live_mask).astype(jnp.bfloat16)
        saved_rows = lax.dynamic_index_in_dim(saved, expert, 1, keepdims=False)
        saved_rows = saved_rows.reshape(DEVICES * CAP, 2 * FF).astype(jnp.float32)
        gate_pre = saved_rows[:, :FF]
        up_pre = saved_rows[:, FF:]
        weight_in = lax.dynamic_index_in_dim(w_in, expert, 0, keepdims=False)
        weight_down = lax.dynamic_index_in_dim(w_down, expert, 0, keepdims=False)
        hidden_grad = jnp.dot(scaled, weight_down.T, preferred_element_type=jnp.float32)
        sigmoid_gate = jax.nn.sigmoid(gate_pre)
        activated = gate_pre * sigmoid_gate
        pre_grad = jnp.concatenate([hidden_grad * up_pre * sigmoid_gate * (1.0 + gate_pre * (1.0 - sigmoid_gate)), hidden_grad * activated], axis=1).astype(jnp.bfloat16)
        hidden = (activated * up_pre).astype(jnp.bfloat16)
        slot_grads = jnp.dot(pre_grad, weight_in.T, preferred_element_type=jnp.float32).astype(jnp.bfloat16)
        in_accum = in_accum.at[tok_index].add(slot_grads.astype(jnp.float32) * live_mask)
        tok_group = tok_rows.reshape(N_DP, N_EXPERT * CAP, D).astype(jnp.float32)
        scaled_group = scaled.reshape(N_DP, N_EXPERT * CAP, D).astype(jnp.float32)
        pre_group = pre_grad.reshape(N_DP, N_EXPERT * CAP, 2 * FF).astype(jnp.float32)
        hidden_group = hidden.reshape(N_DP, N_EXPERT * CAP, FF).astype(jnp.float32)
        grad_in = jnp.einsum('rsd,rsf->rdf', tok_group, pre_group)
        grad_down = jnp.einsum('rsd,rsf->rdf', scaled_group, hidden_group)
        partial_sums = lax.optimization_barrier(jnp.concatenate([grad_in, grad_down], axis=2).astype(jnp.bfloat16)).astype(jnp.float32)
        trained_flag = jnp.any(trained == expert).astype(jnp.float32)
        weight_block = (jnp.sum(partial_sums, axis=0) * trained_flag).astype(jnp.bfloat16)
        return in_accum, weight_block

    in_accum, weight_grad = lax.scan(one_expert, jnp.zeros((TOKENS, D), jnp.float32), jnp.arange(EXPERTS, dtype=jnp.int32))
    return in_accum.astype(jnp.bfloat16), weight_grad
```

```python
import functools

import jax
import jax.numpy as jnp
from jax import lax
from jax.experimental import pallas as pl
from jax.experimental.pallas import tpu as pltpu
from jax.sharding import PartitionSpec as P

AXIS = "expert"
CORES = 2
CONTRACT_LAST = (((1,), (1,)), ((), ()))
CONTRACT_FIRST = (((0,), (0,)), ((), ()))


def chip_cycle(chips):
    width = 1
    while (2 * width) ** 2 <= chips:
        width *= 2
    height = chips // width
    if width == 1:
        return list(range(chips))
    order = [row * width for row in range(height)]
    for back, row in enumerate(reversed(range(height))):
        columns = range(1, width) if back % 2 == 0 else range(width - 1, 0, -1)
        order += [row * width + column for column in columns]
    return order


def row_tile(rows):
    return max(t for t in range(16, 129, 16) if rows % t == 0)


def gather_kernel(js, slot_ref, gate_ref, *refs, count, planes, cap, tile, gated):
    chunks, out_ref, buf, sems = refs[:count], refs[count], refs[count + 1], refs[count + 2]
    block = buf.shape[1] // count
    copies = []
    for i, chunk in enumerate(chunks):
        for plane in range(planes):
            start = pl.multiple_of(js[i] * block, block)
            copies.append(
                pltpu.make_async_copy(
                    chunk.at[pl.ds(plane * block, block)],
                    buf.at[plane, pl.ds(start, block)],
                    sems.at[i, plane],
                )
            )
    for copy in copies:
        copy.start()
    for copy in copies:
        copy.wait()
    rows, width = out_ref.shape[1], out_ref.shape[2]
    for plane in range(planes):
        for first in range(0, rows, tile):
            low, high = first // cap, (first + tile - 1) // cap + 1
            window = slice(low * block, high * block)
            slots = slot_ref[plane : plane + 1, window]
            labels = lax.broadcasted_iota(jnp.int32, (tile, (high - low) * block), 0) + first
            hit = labels == slots
            onehot = hit.astype(jnp.float32).astype(jnp.bfloat16)
            if gated:
                scale = jnp.sum(
                    jnp.where(hit, gate_ref[plane : plane + 1, window], 0.0), axis=1, keepdims=True
                )
            for left in range(0, width, 512):
                values = jnp.dot(
                    onehot, buf[plane, window, left : left + 512], preferred_element_type=jnp.float32
                )
                if gated:
                    values = values * scale
                out_ref[plane, first : first + tile, left : left + 512] = values.astype(jnp.bfloat16)


def gather_rows(js, slots, gates, chunks, rows, cap, gated):
    planes, count = slots.shape[0], len(chunks)
    block, width = chunks[0].shape[0] // planes, chunks[0].shape[1]
    flops = 2 * planes * rows * 4 * block * width
    return pl.pallas_call(
        functools.partial(
            gather_kernel, count=count, planes=planes, cap=cap, tile=row_tile(rows), gated=gated
        ),
        out_shape=jax.ShapeDtypeStruct((planes, rows, width), jnp.bfloat16),
        grid_spec=pltpu.PrefetchScalarGridSpec(
            num_scalar_prefetch=1,
            grid=(1,),
            in_specs=[pl.BlockSpec(slots.shape, lambda i, js: (0, 0))] * 2
            + [pl.BlockSpec(memory_space=pl.ANY)] * count,
            out_specs=pl.BlockSpec((planes, rows, width), lambda i, js: (0, 0, 0)),
            scratch_shapes=[
                pltpu.VMEM((planes, count * block, width), jnp.bfloat16),
                pltpu.SemaphoreType.DMA((count, planes)),
            ],
        ),
        compiler_params=pltpu.CompilerParams(vmem_limit_bytes=40 * 2**20),
        cost_estimate=pl.CostEstimate(
            flops=flops, bytes_accessed=planes * (count * block + rows) * width * 2, transcendentals=0
        ),
        name="gather_rows",
    )(js, slots, gates, *chunks)


def scatter_kernel(js, slot_ref, grad_ref, *refs, count, cap, span):
    outs, buf, sems = refs[:count], refs[count], refs[count + 1]
    block, width = buf.shape[1], buf.shape[2]
    rows = grad_ref.shape[0]
    copies = []
    for i, out in enumerate(outs):
        j = js[i]
        first = pl.multiple_of(jnp.minimum(j * cap // 16 * 16, rows - span), 16)
        slots = slot_ref[pl.ds(j, 1), :]
        labels = lax.broadcasted_iota(jnp.int32, (span, block), 0) + first
        onehot = (labels == slots).astype(jnp.float32).astype(jnp.bfloat16)
        for left in range(0, width, 512):
            values = lax.dot_general(
                onehot,
                grad_ref[pl.ds(first, span), left : left + 512],
                CONTRACT_FIRST,
                preferred_element_type=jnp.float32,
            )
            buf[i, :, left : left + 512] = values.astype(jnp.bfloat16)
        copy = pltpu.make_async_copy(buf.at[i], out, sems.at[i])
        copy.start()
        copies.append(copy)
    for copy in copies:
        copy.wait()


def scatter_rows(js, slots, grads, cap):
    count, block = slots.shape
    rows, width = grads.shape
    span = min(rows, -(-(cap + 15) // 16) * 16)
    return pl.pallas_call(
        functools.partial(scatter_kernel, count=count, cap=cap, span=span),
        out_shape=[jax.ShapeDtypeStruct((block, width), jnp.bfloat16)] * count,
        grid_spec=pltpu.PrefetchScalarGridSpec(
            num_scalar_prefetch=1,
            grid=(1,),
            in_specs=[
                pl.BlockSpec(slots.shape, lambda i, js: (0, 0)),
                pl.BlockSpec(grads.shape, lambda i, js: (0, 0)),
            ],
            out_specs=[pl.BlockSpec(memory_space=pl.ANY)] * count,
            scratch_shapes=[
                pltpu.VMEM((count, block, width), jnp.bfloat16),
                pltpu.SemaphoreType.DMA((count,)),
            ],
        ),
        compiler_params=pltpu.CompilerParams(vmem_limit_bytes=40 * 2**20),
        cost_estimate=pl.CostEstimate(
            flops=2 * count * span * block * width,
            bytes_accessed=(rows + count * block) * width * 2,
            transcendentals=0,
        ),
        name="scatter_rows",
    )(js, slots, grads)


def per_device(tokens, out_grad, expert_ids, gate_weights, trained, w_in, w_down, saved):
    groups, replicas = lax.axis_size(AXIS), lax.axis_size("dp")
    chips = groups // CORES
    tok_count, model_width = tokens.shape
    slot_total = saved.shape[2]
    cap = slot_total // groups
    hidden_units = w_down.shape[1]
    cut = model_width // replicas
    me, replica = lax.axis_index(AXIS), lax.axis_index("dp")

    order = chip_cycle(chips)
    after = {order[i]: order[(i + 1) % chips] for i in range(chips)}
    ahead = [(CORES * c + k, CORES * after[c] + k) for c in range(chips) for k in range(CORES)]
    behind = [(b, a) for a, b in ahead]
    swap = [(i, i ^ 1) for i in range(groups)]
    place = {c: i for i, c in enumerate(order)}
    table = jnp.array(
        [[order[(place[c] + d) % chips] for d in range(chips)] for c in range(chips)], jnp.int32
    )
    chip_at = lax.dynamic_slice(table, (me // CORES, 0), (1, chips))[0]
    core = me % CORES
    js = jnp.concatenate([CORES * chip_at + core, CORES * chip_at + 1 - core])

    def ring_gather(value, far):
        held = {0: value}
        up = down = value
        for step in range(1, max(far, chips - 1 - far) + 1):
            if step <= far:
                up = lax.ppermute(up, AXIS, ahead)
                held[(-step) % chips] = up
            if step <= chips - 1 - far:
                down = lax.ppermute(down, AXIS, behind)
                held[step] = down
        own = [held[d] for d in range(chips)]
        return own + [lax.ppermute(x, AXIS, swap) for x in own]

    def shifted(value, shift):
        return lax.ppermute(value, "dp", [(r, (r + shift) % replicas) for r in range(replicas)])

    def columns(value, owner):
        return lax.dynamic_slice_in_dim(value, owner * cut, cut, 1)

    labels = jnp.arange(groups, dtype=jnp.int32)
    chosen = expert_ids[None, :, :] == labels[:, None, None]
    routed = jnp.any(chosen, axis=2)
    gate = jnp.sum(jnp.where(chosen, gate_weights[None], 0.0), axis=2)
    earlier = jnp.triu(jnp.ones((tok_count, tok_count), jnp.bfloat16), 1)
    rank = jnp.dot(routed.astype(jnp.bfloat16), earlier, preferred_element_type=jnp.float32)
    slot = jnp.where(routed, rank + (me * cap).astype(jnp.float32), -1.0)
    info = lax.all_to_all(
        jnp.stack([slot, gate], axis=1), AXIS, split_axis=0, concat_axis=0, tiled=True
    )
    slots = info[:, 0, :].astype(jnp.int32)
    gates = info[:, 1, :]

    far = chips // 2
    grad_chunks = ring_gather(out_grad, far)
    halves = jnp.concatenate(
        [columns(tokens, replica)]
        + [shifted(columns(tokens, (replica + i) % replicas), i) for i in range(1, replicas)],
        axis=0,
    )
    token_chunks = ring_gather(halves, chips - 1 - far)
    plane_slots = [info[:, 0, :]] + [shifted(info[:, 0, :], i) for i in range(1, replicas)]
    all_slots = jnp.stack(plane_slots).reshape(replicas, groups * tok_count).astype(jnp.int32)

    s = gather_rows(
        js, slots.reshape(1, -1), gates.reshape(1, -1), grad_chunks, slot_total, cap, True
    )[0]
    saved_rows = saved.reshape(slot_total, 2 * hidden_units).astype(jnp.float32)
    gate_pre = saved_rows[:, :hidden_units]
    up_pre = saved_rows[:, hidden_units:]
    hidden_grad = lax.dot_general(s, w_down[0], CONTRACT_LAST, preferred_element_type=jnp.float32)
    sigmoid_gate = jax.nn.sigmoid(gate_pre)
    activated = gate_pre * sigmoid_gate
    pre_grad = jnp.concatenate(
        [
            hidden_grad * up_pre * sigmoid_gate * (1.0 + gate_pre * (1.0 - sigmoid_gate)),
            hidden_grad * activated,
        ],
        axis=1,
    ).astype(jnp.bfloat16)
    hidden = (activated * up_pre).astype(jnp.bfloat16)
    slot_grads = lax.dot_general(
        pre_grad, w_in[0], CONTRACT_LAST, preferred_element_type=jnp.float32
    ).astype(jnp.bfloat16)

    parts = scatter_rows(js, slots, slot_grads, cap)
    total = {}
    for d in sorted(range(chips), key=lambda d: -min(d, chips - d)):
        total[d] = parts[d].astype(jnp.float32) + lax.ppermute(
            parts[chips + d], AXIS, swap
        ).astype(jnp.float32)
    up_hops = chips - 1 - far
    up, down = total[up_hops], total[up_hops + 1]
    for step in range(max(up_hops, chips - 1 - up_hops)):
        if step < up_hops:
            got = lax.ppermute(up.astype(jnp.bfloat16), AXIS, ahead)
            up = got.astype(jnp.float32)
            if step < up_hops - 1:
                up = up + total[up_hops - 1 - step]
        if step < chips - 1 - up_hops:
            got = lax.ppermute(down.astype(jnp.bfloat16), AXIS, behind)
            down = got.astype(jnp.float32)
            if step < chips - 2 - up_hops:
                down = down + total[up_hops + 2 + step]
    in_grad = (total[0] + up + down).astype(jnp.bfloat16)

    def down_part(owner):
        return lax.dot_general(
            hidden, columns(s, owner), CONTRACT_FIRST, preferred_element_type=jnp.float32
        )

    grad_down = down_part(replica)
    grad_in = None
    x = gather_rows(js, all_slots, all_slots.astype(jnp.float32), token_chunks, slot_total, cap, False)
    for i in range(replicas):
        other = pre_grad if i == 0 else shifted(pre_grad, i)
        part = lax.dot_general(other, x[i], CONTRACT_FIRST, preferred_element_type=jnp.float32)
        grad_in = part if grad_in is None else grad_in + part
        if i:
            sent = down_part((replica + i) % replicas).astype(jnp.bfloat16)
            grad_down = grad_down + shifted(sent, i).astype(jnp.float32)
    trained_flag = jnp.any(trained == me).astype(jnp.float32)
    weight = (jnp.concatenate([grad_in, grad_down], axis=0) * trained_flag).astype(jnp.bfloat16)
    return in_grad, weight.T[None]


def solution(mesh):
    return jax.shard_map(
        per_device,
        mesh=mesh,
        in_specs=(
            P(("dp", "expert"), None),
            P(("dp", "expert"), None),
            P(("dp", "expert"), None),
            P(("dp", "expert"), None),
            P(),
            P("expert", None, None),
            P("expert", None, None),
            P("dp", "expert", None, None),
        ),
        out_specs=(P(("dp", "expert"), None), P("expert", "dp", None)),
        check_vma=False,
    )
```

```python
import functools

import jax
import jax.numpy as jnp
from jax import lax
from jax.experimental import pallas as pl
from jax.experimental.pallas import tpu as pltpu
from jax.sharding import PartitionSpec as P

AXIS = "expert"
CORES = 2
CONTRACT_LAST = (((1,), (1,)), ((), ()))
CONTRACT_FIRST = (((0,), (0,)), ((), ()))


def chip_cycle(chips):
    width = 1
    while (2 * width) ** 2 <= chips:
        width *= 2
    height = chips // width
    if width == 1:
        return list(range(chips))
    order = [row * width for row in range(height)]
    for back, row in enumerate(reversed(range(height))):
        columns = range(1, width) if back % 2 == 0 else range(width - 1, 0, -1)
        order += [row * width + column for column in columns]
    return order


def after_all(*values):
    return lax.optimization_barrier(values)


def split_rows(value, count):
    tiles = value.shape[0] // 8
    ends = [8 * (tiles * (i + 1) // count) for i in range(count - 1)] + [value.shape[0]]
    return [value[a:b] for a, b in zip([0] + ends[:-1], ends)]


def windows(rows, cap, devices, group):
    span = min(rows, -(-(group * cap + 15) // 16) * 16)
    return [min(d * cap // 16 * 16, rows - span) for d in range(0, devices, group)], span


def gather_kernel(js, slot_ref, gate_ref, *refs, count, planes, cap, group, gated):
    chunks, out_hbm, buf, out_ref, in_sems, out_sems = refs[:count], *refs[count:]
    block = buf.shape[1] // count
    rows, width = out_ref.shape[1], out_ref.shape[2]
    for plane in range(planes):
        for i, chunk in enumerate(chunks):
            start = pl.multiple_of(js[i] * block, block)
            pltpu.make_async_copy(
                chunk.at[pl.ds(plane * block, block)],
                buf.at[plane, pl.ds(start, block)],
                in_sems.at[plane, js[i]],
            ).start()
    firsts, span = windows(rows, cap, count, group)
    firsts = firsts + [rows]
    copies = []
    for plane in range(planes):
        done = 0
        for g in range(count // group):
            first = firsts[g]
            for j in range(g * group, (g + 1) * group):
                window = buf.at[plane, pl.ds(j * block, block)]
                pltpu.make_async_copy(window, window, in_sems.at[plane, j]).wait()
            window = slice(g * group * block, (g + 1) * group * block)
            labels = lax.broadcasted_iota(jnp.int32, (span, group * block), 0) + first
            hit = labels == slot_ref[plane : plane + 1, window]
            onehot = hit.astype(jnp.float32).astype(jnp.bfloat16)
            if gated:
                gates = gate_ref[plane : plane + 1, window]
                scale = jnp.sum(jnp.where(hit, gates, 0.0), axis=1, keepdims=True)
            again = max(0, done - first)
            for left in range(0, width, 512):
                lanes = slice(left, left + 512)
                values = jnp.dot(
                    onehot, buf[plane, window, lanes], preferred_element_type=jnp.float32
                )
                if gated:
                    values = values * scale
                values = values.astype(jnp.bfloat16)
                if again:
                    out_ref[plane, first : first + again, lanes] += values[:again]
                if again < span:
                    out_ref[plane, first + again : first + span, lanes] = values[again:]
            done = first + span
            place = pl.ds(first, firsts[g + 1] - first)
            copy = pltpu.make_async_copy(
                out_ref.at[plane, place], out_hbm.at[plane, place], out_sems.at[plane, g]
            )
            copy.start()
            copies.append(copy)
    for copy in copies:
        copy.wait()


def gather_rows(js, slots, gates, chunks, rows, cap, gated):
    planes, count, group = slots.shape[0], len(chunks), CORES
    block, width = chunks[0].shape[0] // planes, chunks[0].shape[1]
    return pl.pallas_call(
        functools.partial(
            gather_kernel, count=count, planes=planes, cap=cap, group=group, gated=gated
        ),
        out_shape=jax.ShapeDtypeStruct((planes, rows, width), jnp.bfloat16),
        grid_spec=pltpu.PrefetchScalarGridSpec(
            num_scalar_prefetch=1,
            grid=(1,),
            in_specs=[pl.BlockSpec(slots.shape, lambda i, js: (0, 0))] * 2
            + [pl.BlockSpec(memory_space=pl.ANY)] * count,
            out_specs=pl.BlockSpec(memory_space=pltpu.HBM),
            scratch_shapes=[
                pltpu.VMEM((planes, count * block, width), jnp.bfloat16),
                pltpu.VMEM((planes, rows, width), jnp.bfloat16),
                pltpu.SemaphoreType.DMA((planes, count)),
                pltpu.SemaphoreType.DMA((planes, count // group)),
            ],
        ),
        compiler_params=pltpu.CompilerParams(vmem_limit_bytes=58 * 2**20),
        cost_estimate=pl.CostEstimate(
            flops=0,
            bytes_accessed=2 * planes * (count * block + rows) * width * 2,
            transcendentals=0,
        ),
        name="gather_rows",
    )(js, slots, gates, *chunks)


def scatter_kernel(js, slot_ref, grad_ref, *refs, groups, cap, span):
    outs, buf, sems = refs[:-2], refs[-2], refs[-1]
    block, width = buf.shape[1], buf.shape[2]
    rows, listed = grad_ref.shape[0], sum(groups)
    copies, x = [], 0
    for g, size in enumerate(groups):
        for at in range(size):
            for side in range(CORES):
                i = side * listed + x
                j = js[i]
                first = pl.multiple_of(jnp.minimum(j * cap // 16 * 16, rows - span), 16)
                slots = slot_ref[pl.ds(j, 1), :]
                labels = lax.broadcasted_iota(jnp.int32, (span, block), 0) + first
                onehot = (labels == slots).astype(jnp.float32).astype(jnp.bfloat16)
                for left in range(0, width, 512):
                    values = lax.dot_general(
                        onehot,
                        grad_ref[pl.ds(first, span), left : left + 512],
                        CONTRACT_FIRST,
                        preferred_element_type=jnp.float32,
                    )
                    buf[i, :, left : left + 512] = values.astype(jnp.bfloat16)
                out = outs[CORES * g + side].at[pl.ds(at * block, block)]
                copies.append(pltpu.make_async_copy(buf.at[i], out, sems.at[i]))
                copies[-1].start()
            x += 1
    for copy in copies:
        copy.wait()


def scatter_rows(js, slots, grads, cap, groups):
    count, block = slots.shape
    rows, width = grads.shape
    span = min(rows, -(-(cap + 15) // 16) * 16)
    return pl.pallas_call(
        functools.partial(scatter_kernel, groups=groups, cap=cap, span=span),
        out_shape=[
            jax.ShapeDtypeStruct((size * block, width), jnp.bfloat16)
            for size in groups
            for side in range(CORES)
        ],
        grid_spec=pltpu.PrefetchScalarGridSpec(
            num_scalar_prefetch=1,
            grid=(1,),
            in_specs=[
                pl.BlockSpec(slots.shape, lambda i, js: (0, 0)),
                pl.BlockSpec(grads.shape, lambda i, js: (0, 0)),
            ],
            out_specs=[pl.BlockSpec(memory_space=pltpu.HBM)] * (CORES * len(groups)),
            scratch_shapes=[
                pltpu.VMEM((count, block, width), jnp.bfloat16),
                pltpu.SemaphoreType.DMA((count,)),
            ],
        ),
        compiler_params=pltpu.CompilerParams(vmem_limit_bytes=58 * 2**20),
        cost_estimate=pl.CostEstimate(
            flops=2 * count * span * block * width,
            bytes_accessed=2 * (rows + count * block) * width * 2,
            transcendentals=0,
        ),
        name="scatter_rows",
    )(js, slots, grads)


def per_device(tokens, out_grad, expert_ids, gate_weights, trained, w_in, w_down, saved):
    groups, replicas = lax.axis_size(AXIS), lax.axis_size("dp")
    chips = groups // CORES
    tok_count, model_width = tokens.shape
    slot_total = saved.shape[2]
    cap = slot_total // groups
    hidden_units = w_down.shape[1]
    cut = model_width // replicas
    me, replica = lax.axis_index(AXIS), lax.axis_index("dp")
    shifts = range(1, replicas)

    far = chips // 2
    order = chip_cycle(chips)
    place = {c: i for i, c in enumerate(order)}

    def at(device, steps):
        return order[(place[device // CORES] + (steps if device % CORES == 0 else -steps)) % chips]

    along = [(i, CORES * at(i, 1) + i % CORES) for i in range(groups)]
    across = [(i, CORES * at(i, 1) + 1 - i % CORES) for i in range(groups)]
    swap = [(i, i ^ 1) for i in range(groups)]
    names = [("a", 0), ("b", 0)]
    names += [(kind, i) for i in range(1, far + 1) for kind in "ab" if (kind, i) != ("b", far)]
    pairs = names[:1] + names[2:]

    def device_at(device, name, way):
        kind, steps = name
        return CORES * at(device, way * steps) + (device % CORES if kind == "a" else 1 - device % CORES)

    def listing(labels, way):
        table = [
            [device_at(i, name, way) for name in labels]
            + [device_at(i ^ 1, name, way) for name in labels]
            for i in range(groups)
        ]
        return lax.dynamic_slice(jnp.array(table, jnp.int32), (me, 0), (1, 2 * len(labels)))[0]

    leaving = pairs[:0:-1]
    leaving = sorted(leaving, key=lambda name: (-name[1], name[0] == "a")) + [("a", 0)]
    sizes = [1, 2, len(leaving) - 3]
    work = {"js": listing(pairs, -1), "leaving": listing(leaving, 1)}

    def shifted(value, shift):
        return lax.ppermute(value, "dp", [(r, (r + shift) % replicas) for r in range(replicas)])

    def columns(value, owner):
        return lax.dynamic_slice_in_dim(value, owner * cut, cut, 1)

    def together(*places):
        values = after_all(*[box[key] for box, key in places])
        for (box, key), value in zip(places, values):
            box[key] = value

    came = {}

    def send(pieces, label, i):
        for shift in shifts:
            came[label, i, shift] = shifted(pieces[i], shift)
        return [(came, (label, i, shift)) for shift in shifts]

    def whole(label, count, shift):
        return jnp.concatenate([came[label, i, shift] for i in range(count)], axis=0)

    def hop(blocks, kind, step):
        blocks[kind, step] = lax.ppermute(blocks[kind, step - 1], AXIS, along)
        return blocks, (kind, step)

    def exchange(blocks, name):
        blocks["other", name] = lax.ppermute(blocks[name], AXIS, swap)
        return blocks, ("other", name)

    def all_blocks(blocks):
        return [blocks[name] for name in pairs] + [blocks["other", name] for name in pairs]

    labels = jnp.arange(groups, dtype=jnp.int32)
    chosen = expert_ids[None, :, :] == labels[:, None, None]
    routed = jnp.any(chosen, axis=2)
    gate = jnp.sum(jnp.where(chosen, gate_weights[None], 0.0), axis=2)
    earlier = jnp.triu(jnp.ones((tok_count, tok_count), jnp.bfloat16), 1)
    rank = jnp.dot(routed.astype(jnp.bfloat16), earlier, preferred_element_type=jnp.float32)
    slot = jnp.where(routed, rank + (me * cap).astype(jnp.float32), -1.0)
    listed = [gate, slot] + [shifted(slot, i) for i in shifts]
    halves = [columns(tokens, (replica + i) % replicas) for i in range(replicas)]
    work["halves"] = jnp.concatenate(
        [halves[0]] + [shifted(halves[i], i) for i in shifts], axis=0
    )
    saved_rows = saved.reshape(slot_total, 2 * hidden_units)
    gate_pre, up_pre = saved_rows[:, :hidden_units], saved_rows[:, hidden_units:]
    saved_pieces = split_rows(saved_rows, 2)

    grads = {("a", 0): out_grad}
    grads["b", 0] = exchange(grads, ("a", 0))[0]["other", ("a", 0)]
    for step in range(1, far + 1):
        moved = [hop(grads, "a", step)]
        if step < far:
            hop(grads, "b", step)
        if step == 2:
            moved += [(work, key) for key in ("js", "leaving", "halves")]
        elif step == 3:
            moved += [exchange(grads, (kind, 1)) for kind in "ab"]
        elif step == far:
            moved += [exchange(grads, (kind, 2)) for kind in "ab"]
            work["gates"] = work["info"][:, 0, :].reshape(1, -1)
            all_slots = jnp.swapaxes(work["info"][:, 1:, :], 0, 1).astype(jnp.int32)
            work["slots"] = all_slots.reshape(replicas, -1)
            work["own"] = all_slots[0]
            moved += [(work, key) for key in ("gates", "slots", "own")]
            moved += send(saved_pieces, "saved", 0)
        together(*moved)
        if step == 1:
            work["info"] = lax.all_to_all(
                jnp.stack(listed, axis=1), AXIS, split_axis=0, concat_axis=0, tiled=True
            )
        elif step == far - 1:
            together((work, "info"), (grads, ("b", step)))
    held = {("a", 0): work["halves"]}
    held["b", 0] = exchange(held, ("a", 0))[0]["other", ("a", 0)]
    together((held, ("a", 0)), (grads, ("b", far - 1)))
    for step in range(1, far + 1):
        hop(held, "a", step)
        if step < far:
            hop(held, "b", step)
    for blocks in (grads, held):
        for name in pairs:
            if ("other", name) not in blocks:
                exchange(blocks, name)
    js, gates, all_slots = work["js"], work["gates"], work["slots"]

    def pre_grads(hidden_grad, gate_pre, up_pre):
        gate_pre, up_pre = gate_pre.astype(jnp.float32), up_pre.astype(jnp.float32)
        sigmoid_gate = jax.nn.sigmoid(gate_pre)
        activated = gate_pre * sigmoid_gate
        gate_grad = hidden_grad * up_pre * sigmoid_gate * (1.0 + gate_pre * (1.0 - sigmoid_gate))
        up_grad = hidden_grad * activated
        hidden = activated * up_pre
        return [value.astype(jnp.bfloat16) for value in (gate_grad, up_grad, hidden)]

    def down_part(owner):
        return lax.dot_general(
            hidden, columns(s, owner), CONTRACT_FIRST, preferred_element_type=jnp.float32
        )

    s = gather_rows(js, all_slots[:1], gates, all_blocks(grads), slot_total, cap, True)[0]
    hidden_grad = lax.dot_general(s, w_down[0], CONTRACT_LAST, preferred_element_type=jnp.float32)
    gate_grad, up_grad, hidden = pre_grads(hidden_grad, gate_pre, up_pre)
    hidden_pieces = split_rows(hidden_grad.astype(jnp.bfloat16), 2)
    work["pre_grad"] = jnp.concatenate([gate_grad, up_grad], axis=1)
    together((work, "pre_grad"), *send(saved_pieces, "saved", 1))
    slot_grads = lax.dot_general(
        work["pre_grad"], w_in[0], CONTRACT_LAST, preferred_element_type=jnp.float32
    ).astype(jnp.bfloat16)
    parts = scatter_rows(work["leaving"], work["own"], slot_grads, cap, sizes)
    kept, sent = parts[::CORES], parts[1::CORES]
    others = [down_part((replica + i) % replicas).astype(jnp.bfloat16) for i in shifts]
    swapped = [lax.ppermute(value, AXIS, swap) for value in sent]
    moved = [(swapped, 0), (held, ("a", far)), (held, ("b", far - 1))]
    together(*moved, *send(hidden_pieces, "hidden", 0))

    def total(name):
        g, row = 0, leaving.index(name)
        while row >= sizes[g]:
            g, row = g + 1, row - sizes[g]
        values = [
            lax.slice_in_dim(x[g], row * tok_count, (row + 1) * tok_count) for x in (kept, swapped)
        ]
        return values[0].astype(jnp.float32) + values[1].astype(jnp.float32)

    def over_slots(values):
        return sum(
            lax.dot_general(values[i], x[i], CONTRACT_FIRST, preferred_element_type=jnp.float32)
            for i in range(replicas)
        )

    down_pieces = [split_rows(other, 3) for other in others]
    sums = {}
    for n, (kind, steps) in enumerate(leaving[:-1]):
        value = total((kind, steps))
        if (kind, steps + 1) in sums:
            value = value + sums[kind, steps + 1].astype(jnp.float32)
        last = (kind, steps) == ("b", 1)
        sums[kind, steps] = lax.ppermute(
            value.astype(jnp.bfloat16), AXIS, across if last else along
        )
        if n == 1:
            together((sums, (kind, steps)), *send(hidden_pieces, "hidden", 1))
        elif n in (3, 5):
            for i in shifts:
                came["down", n // 2 - 1, i] = shifted(down_pieces[i - 1][n // 2 - 1], i)
                together((sums, (kind, steps)), (came, ("down", n // 2 - 1, i)))
    for i in shifts:
        came["down", 2, i] = shifted(down_pieces[i - 1][2], i)

    x = gather_rows(
        js, all_slots, all_slots.astype(jnp.float32), all_blocks(held), slot_total, cap, False
    )
    gate_grads, up_grads = [gate_grad], [up_grad]
    for i in shifts:
        other = whole("saved", 2, i)
        other = pre_grads(
            whole("hidden", 2, i).astype(jnp.float32),
            other[:, :hidden_units],
            other[:, hidden_units:],
        )
        gate_grads.append(other[0])
        up_grads.append(other[1])
    grad_down = down_part(replica)
    for i in shifts:
        grad_down = grad_down + whole("down", 3, i).astype(jnp.float32)
    weight = jnp.concatenate([over_slots(gate_grads), over_slots(up_grads), grad_down], axis=0)
    trained_flag = jnp.any(trained == me).astype(jnp.float32)
    work["weight"] = (weight * trained_flag).astype(jnp.bfloat16)
    together((work, "weight"), (sums, ("a", 1)))
    in_grad = total(("a", 0)) + sums["a", 1].astype(jnp.float32)
    if far > 1:
        in_grad = in_grad + sums["b", 1].astype(jnp.float32)
    return in_grad.astype(jnp.bfloat16), work["weight"].T[None]


def solution(mesh):
    return jax.shard_map(
        per_device,
        mesh=mesh,
        in_specs=(
            P(("dp", "expert"), None),
            P(("dp", "expert"), None),
            P(("dp", "expert"), None),
            P(("dp", "expert"), None),
            P(),
            P("expert", None, None),
            P("expert", None, None),
            P("dp", "expert", None, None),
        ),
        out_specs=(P(("dp", "expert"), None), P("expert", "dp", None)),
        check_vma=False,
    )
```

```python
import functools

import jax
import jax.numpy as jnp
from jax import lax
from jax.experimental import pallas as pl
from jax.experimental.pallas import tpu as pltpu
from jax.sharding import PartitionSpec as P

AXIS = "expert"
CORES = 2
CONTRACT_LAST = (((1,), (1,)), ((), ()))
CONTRACT_FIRST = (((0,), (0,)), ((), ()))


def chip_cycle(chips):
    width = 1
    while (2 * width) ** 2 <= chips:
        width *= 2
    height = chips // width
    if width == 1:
        return list(range(chips))
    order = [row * width for row in range(height)]
    for back, row in enumerate(reversed(range(height))):
        columns = range(1, width) if back % 2 == 0 else range(width - 1, 0, -1)
        order += [row * width + column for column in columns]
    return order


def after_all(*values):
    return lax.optimization_barrier(values)


def ahead_by(value, microseconds, after=()):
    return pl.pallas_call(
        lambda *refs: None,
        out_shape=jax.ShapeDtypeStruct(value.shape, value.dtype),
        in_specs=[pl.BlockSpec(memory_space=pltpu.HBM)] + [pl.BlockSpec(memory_space=pl.ANY)] * len(after),
        out_specs=pl.BlockSpec(memory_space=pltpu.HBM),
        input_output_aliases={0: 0},
        cost_estimate=pl.CostEstimate(
            flops=0, bytes_accessed=int(microseconds * 3.0e6), transcendentals=0
        ),
        name="ahead_by",
    )(value, *after)


def split_rows(value, count, tile=16):
    tiles = value.shape[0] // tile
    ends = [tile * (tiles * (i + 1) // count) for i in range(count - 1)] + [value.shape[0]]
    return [value[a:b] for a, b in zip([0] + ends[:-1], ends)]


def windows(rows, cap, devices, group):
    span = min(rows, -(-(group * cap + 15) // 16) * 16)
    return [min(d * cap // 16 * 16, rows - span) for d in range(0, devices, group)], span


def gather_kernel(js, slot_ref, gate_ref, *refs, count, planes, cap, group, gated):
    chunks, (out_hbm, buf, out_ref, in_sems, out_sems) = refs[:-5], refs[-5:]
    block = buf.shape[1] // count
    rows, width = out_ref.shape[1], out_ref.shape[2]
    blocks = [
        chunk.at[pl.ds(first, planes * block)]
        for chunk in chunks
        for first in range(0, chunk.shape[0], planes * block)
    ]
    for plane in range(planes):
        for i, source in enumerate(blocks):
            start = pl.multiple_of(js[i] * block, block)
            pltpu.make_async_copy(
                source.at[pl.ds(plane * block, block)],
                buf.at[plane, pl.ds(start, block)],
                in_sems.at[plane, js[i]],
            ).start()
    firsts, span = windows(rows, cap, count, group)
    firsts = firsts + [rows]
    copies = []
    for plane in range(planes):
        done = 0
        for g in range(count // group):
            first = firsts[g]
            for j in range(g * group, (g + 1) * group):
                window = buf.at[plane, pl.ds(j * block, block)]
                pltpu.make_async_copy(window, window, in_sems.at[plane, j]).wait()
            window = slice(g * group * block, (g + 1) * group * block)
            labels = lax.broadcasted_iota(jnp.int32, (span, group * block), 0) + first
            hit = labels == slot_ref[plane : plane + 1, window]
            onehot = hit.astype(jnp.float32).astype(jnp.bfloat16)
            if gated:
                gates = gate_ref[plane : plane + 1, window]
                scale = jnp.sum(jnp.where(hit, gates, 0.0), axis=1, keepdims=True)
            again = max(0, done - first)
            for left in range(0, width, 512):
                lanes = slice(left, left + 512)
                values = jnp.dot(
                    onehot, buf[plane, window, lanes], preferred_element_type=jnp.float32
                )
                if gated:
                    values = values * scale
                values = values.astype(jnp.bfloat16)
                if again:
                    out_ref[plane, first : first + again, lanes] += values[:again]
                if again < span:
                    out_ref[plane, first + again : first + span, lanes] = values[again:]
            done = first + span
            place = pl.ds(first, firsts[g + 1] - first)
            copy = pltpu.make_async_copy(
                out_ref.at[plane, place], out_hbm.at[plane, place], out_sems.at[plane, g]
            )
            copy.start()
            copies.append(copy)
    for copy in copies:
        copy.wait()


def gather_rows(js, slots, gates, chunks, rows, cap, gated):
    planes, count, group = slots.shape[0], js.shape[0], CORES
    block, width = slots.shape[1] // count, chunks[0].shape[1]
    return pl.pallas_call(
        functools.partial(
            gather_kernel, count=count, planes=planes, cap=cap, group=group, gated=gated
        ),
        out_shape=jax.ShapeDtypeStruct((planes, rows, width), jnp.bfloat16),
        grid_spec=pltpu.PrefetchScalarGridSpec(
            num_scalar_prefetch=1,
            grid=(1,),
            in_specs=[pl.BlockSpec(slots.shape, lambda i, js: (0, 0))] * 2
            + [pl.BlockSpec(memory_space=pl.ANY)] * len(chunks),
            out_specs=pl.BlockSpec(memory_space=pltpu.HBM),
            scratch_shapes=[
                pltpu.VMEM((planes, count * block, width), jnp.bfloat16),
                pltpu.VMEM((planes, rows, width), jnp.bfloat16),
                pltpu.SemaphoreType.DMA((planes, count)),
                pltpu.SemaphoreType.DMA((planes, count // group)),
            ],
        ),
        compiler_params=pltpu.CompilerParams(vmem_limit_bytes=58 * 2**20),
        cost_estimate=pl.CostEstimate(
            flops=0,
            bytes_accessed=int(2 * planes * (count * block + rows) * width * 2),
            transcendentals=0,
        ),
        name="gather_rows",
    )(js, slots, gates, *chunks)


def scatter_kernel(js, slot_ref, grad_ref, *refs, sizes, cap, span):
    outs, buf, sems = refs[:-2], refs[-2], refs[-1]
    count, block, width = buf.shape
    rows = grad_ref.shape[0]
    listed = count // CORES
    copies = []
    places = [(n, at) for n, size in enumerate(sizes) for at in range(size)]
    for order in range(count):
        x, side = order // CORES, order % CORES
        i, (n, at) = x + side * listed, places[x]
        j = js[i]
        first = pl.multiple_of(jnp.minimum(j * cap // 16 * 16, rows - span), 16)
        slots = slot_ref[pl.ds(j, 1), :]
        labels = lax.broadcasted_iota(jnp.int32, (span, block), 0) + first
        onehot = (labels == slots).astype(jnp.float32).astype(jnp.bfloat16)
        for left in range(0, width, 512):
            values = lax.dot_general(
                onehot,
                grad_ref[pl.ds(first, span), left : left + 512],
                CONTRACT_FIRST,
                preferred_element_type=jnp.float32,
            )
            buf[i, :, left : left + 512] = values.astype(jnp.bfloat16)
        out = outs[n + side * len(sizes)].at[pl.ds(at * block, block)]
        copies.append(pltpu.make_async_copy(buf.at[i], out, sems.at[i]))
        copies[-1].start()
    for copy in copies:
        copy.wait()


def scatter_rows(js, slots, grads, cap, sizes):
    count, block = slots.shape
    rows, width = grads.shape
    span = min(rows, -(-(cap + 15) // 16) * 16)
    return pl.pallas_call(
        functools.partial(scatter_kernel, sizes=sizes, cap=cap, span=span),
        out_shape=[jax.ShapeDtypeStruct((n * block, width), jnp.bfloat16) for n in sizes] * CORES,
        grid_spec=pltpu.PrefetchScalarGridSpec(
            num_scalar_prefetch=1,
            grid=(1,),
            in_specs=[
                pl.BlockSpec(slots.shape, lambda i, js: (0, 0)),
                pl.BlockSpec(grads.shape, lambda i, js: (0, 0)),
            ],
            out_specs=[pl.BlockSpec(memory_space=pltpu.HBM)] * (CORES * len(sizes)),
            scratch_shapes=[
                pltpu.VMEM((count, block, width), jnp.bfloat16),
                pltpu.SemaphoreType.DMA((count,)),
            ],
        ),
        compiler_params=pltpu.CompilerParams(vmem_limit_bytes=58 * 2**20),
        cost_estimate=pl.CostEstimate(
            flops=2 * count * span * block * width,
            bytes_accessed=int(2 * (rows + count * block) * width * 2),
            transcendentals=0,
        ),
        name="scatter_rows",
    )(js, slots, grads)


def per_device(tokens, out_grad, expert_ids, gate_weights, trained, w_in, w_down, saved):
    groups, replicas = lax.axis_size(AXIS), lax.axis_size("dp")
    chips = groups // CORES
    tok_count, model_width = tokens.shape
    slot_total = saved.shape[2]
    cap = slot_total // groups
    hidden_units = w_down.shape[1]
    cut = model_width // replicas
    me, replica = lax.axis_index(AXIS), lax.axis_index("dp")
    shifts = range(1, replicas)

    far = chips // 2
    order = chip_cycle(chips)
    place = {c: i for i, c in enumerate(order)}

    def at(device, steps):
        return order[(place[device // CORES] + (steps if device % CORES == 0 else -steps)) % chips]

    along = [(i, CORES * at(i, 1) + i % CORES) for i in range(groups)]
    across = [(i, CORES * at(i, 1) + 1 - i % CORES) for i in range(groups)]
    swap = [(i, i ^ 1) for i in range(groups)]
    names = [("a", 0), ("b", 0)]
    names += [(kind, i) for i in range(1, far + 1) for kind in "ab" if (kind, i) != ("b", far)]
    pairs = names[:1] + names[2:]

    def device_at(device, name, way):
        kind, steps = name
        return CORES * at(device, way * steps) + (device % CORES if kind == "a" else 1 - device % CORES)

    def listing(own, other, way):
        table = [
            [device_at(i, name, way) for name in own] + [device_at(i ^ 1, name, way) for name in other]
            for i in range(groups)
        ]
        size = len(own) + len(other)
        return lax.dynamic_slice(jnp.array(table, jnp.int32), (me, 0), (1, size))[0]

    leaving = [("a", far)] + [(kind, i) for i in range(far - 1, 0, -1) for kind in "ab"] + [("a", 0)]
    sizes = [1] + [2] * (far - 1) + [1]
    work = {
        "js": listing(pairs, pairs, -1),
        "joint": listing(names, names[2:], -1),
        "leaving": listing(leaving, leaving, 1),
    }

    def shifted(value, shift):
        return lax.ppermute(value, "dp", [(r, (r + shift) % replicas) for r in range(replicas)])

    def columns(value, owner):
        return lax.dynamic_slice_in_dim(value, owner * cut, cut, 1)

    def together(*places):
        values = after_all(*[box[key] for box, key in places])
        for (box, key), value in zip(places, values):
            box[key] = value

    came = {}

    def send(pieces, label, i, early):
        for shift in shifts:
            value = shifted(pieces[i], shift)
            came[label, i, shift] = ahead_by(value, early) if early else value
        return [(came, (label, i, shift)) for shift in shifts]

    def whole(label, count, shift):
        return jnp.concatenate([came[label, i, shift] for i in range(count)], axis=0)

    def hop(blocks, kind, step):
        blocks[kind, step] = lax.ppermute(blocks[kind, step - 1], AXIS, along)
        return blocks, (kind, step)

    def exchange(blocks, name):
        blocks["other", name] = lax.ppermute(blocks[name], AXIS, swap)
        return blocks, ("other", name)

    def all_blocks(blocks):
        return [blocks[name] for name in pairs] + [blocks["other", name] for name in pairs]

    labels = jnp.arange(groups, dtype=jnp.int32)
    chosen = expert_ids[None, :, :] == labels[:, None, None]
    routed = jnp.any(chosen, axis=2)
    gate = jnp.sum(jnp.where(chosen, gate_weights[None], 0.0), axis=2)
    earlier = jnp.triu(jnp.ones((tok_count, tok_count), jnp.bfloat16), 1)
    rank = jnp.dot(routed.astype(jnp.bfloat16), earlier, preferred_element_type=jnp.float32)
    slot = jnp.where(routed, rank + (me * cap).astype(jnp.float32), -1.0)
    listed = [gate, slot] + [shifted(slot, i) for i in shifts]
    halves = [columns(tokens, (replica + i) % replicas) for i in range(replicas)]
    work["halves"] = jnp.concatenate(
        [halves[0]] + [shifted(halves[i], i) for i in shifts], axis=0
    )
    own_rows = saved.reshape(slot_total, 2 * hidden_units)
    gate_pre, up_pre = own_rows[:, :hidden_units], own_rows[:, hidden_units:]
    work["saved"] = own_rows

    grads = {("a", 0): out_grad}
    grads["b", 0] = exchange(grads, ("a", 0))[0]["other", ("a", 0)]
    for step in range(1, far + 1):
        moved = [hop(grads, "a", step)]
        if step < far:
            hop(grads, "b", step)
        if step == 1:
            moved += [(listed, -1), (work, "halves"), (work, "saved")]
        elif step == 2:
            moved += [(work, key) for key in ("js", "joint", "leaving", "saved")]
        elif step == 3:
            moved += [exchange(grads, (kind, 1)) for kind in "ab"] + [(saved_pieces, 1)]
        elif step == far:
            moved += [exchange(grads, (kind, 2)) for kind in "ab"]
            work["gates"] = work["info"][:, 0, :].reshape(1, -1)
            all_slots = jnp.swapaxes(work["info"][:, 1:, :], 0, 1).astype(jnp.int32)
            work["slots"] = all_slots.reshape(replicas, -1)
            work["own"] = all_slots[0]
            moved += [(work, key) for key in ("gates", "slots", "own")]
        together(*moved)
        if step == 2:
            saved_pieces[1] = work["saved"][:, hidden_units:]
        if step == 1:
            saved_pieces = [work["saved"][:, :hidden_units], None]
            work["info"] = lax.all_to_all(
                jnp.stack(listed, axis=1), AXIS, split_axis=0, concat_axis=0, tiled=True
            )
        elif step == far - 1:
            together((work, "info"), (grads, ("b", step)))
    held = {("a", 0): work["halves"]}
    exchange(held, ("a", 0))
    held["ab", 0] = jnp.concatenate([held["a", 0], held["other", ("a", 0)]], axis=0)
    together((held, ("ab", 0)), (grads, ("b", far - 1)), *send(saved_pieces, "saved", 0, 12))
    grads["a", far] = ahead_by(grads["a", far], 14)
    for name in pairs:
        if ("other", name) not in grads:
            exchange(grads, name)
    hop(held, "ab", 1)
    js, gates, all_slots = work["js"], work["gates"], work["slots"]

    def pre_grads(hidden_grad, gate_pre, up_pre):
        gate_pre, up_pre = gate_pre.astype(jnp.float32), up_pre.astype(jnp.float32)
        sigmoid_gate = jax.nn.sigmoid(gate_pre)
        activated = gate_pre * sigmoid_gate
        gate_grad = hidden_grad * up_pre * sigmoid_gate * (1.0 + gate_pre * (1.0 - sigmoid_gate))
        up_grad = hidden_grad * activated
        hidden = activated * up_pre
        return [value.astype(jnp.bfloat16) for value in (gate_grad, up_grad, hidden)]

    def down_part(owner):
        return lax.dot_general(
            hidden, columns(s, owner), CONTRACT_FIRST, preferred_element_type=jnp.float32
        )

    work["s"] = gather_rows(js, all_slots[:1], gates, all_blocks(grads), slot_total, cap, True)[0]
    together((work, "s"), (held, ("ab", 1)))
    s = work["s"]
    hidden_grad = lax.dot_general(s, w_down[0], CONTRACT_LAST, preferred_element_type=jnp.float32)
    gate_grad, up_grad, hidden = pre_grads(hidden_grad, gate_pre, up_pre)
    hidden_pieces = split_rows(hidden_grad.astype(jnp.bfloat16), 2, 8)
    work["slot_grads"] = lax.dot_general(
        jnp.concatenate([gate_grad, up_grad], axis=1), w_in[0], CONTRACT_LAST, preferred_element_type=jnp.float32
    ).astype(jnp.bfloat16)
    moved = [hop(held, "ab", 2)]
    together((work, "slot_grads"), *moved)
    parts = scatter_rows(work["leaving"], work["own"], work["slot_grads"], cap, sizes)
    for i in range(len(parts)):
        work["part", i] = parts[i]
    moved = [(work, ("part", i)) for i in range(len(parts))] + send(saved_pieces, "saved", 1, 14)
    together(*moved, hop(held, "ab", 3))
    parts = [work["part", i] for i in range(len(parts))]
    for step in range(4, far):
        hop(held, "ab", step)
    held["a", far] = lax.ppermute(
        lax.slice_in_dim(held["ab", far - 1], 0, replicas * tok_count), AXIS, along
    )
    kept, sent = parts[: len(sizes)], parts[len(sizes) :]
    others = [down_part((replica + i) % replicas).astype(jnp.bfloat16) for i in shifts]
    work["down"] = down_part(replica).astype(jnp.bfloat16)
    swapped = [lax.ppermute(value, AXIS, swap) for value in sent]

    def total(n):
        return kept[n].astype(jnp.float32) + swapped[n].astype(jnp.float32)

    def over_slots(values):
        return sum(
            lax.dot_general(values[i], x[i], CONTRACT_FIRST, preferred_element_type=jnp.float32)
            for i in range(replicas)
        )

    sums = {}
    for n in range(far):
        value = total(n)
        if n == 1:
            value = value + jnp.pad(sums["sum"].astype(jnp.float32), ((0, tok_count), (0, 0)))
        elif n:
            value = value + sums["sum"].astype(jnp.float32)
        value = value.astype(jnp.bfloat16)
        if n < far - 1:
            sums["sum"] = lax.ppermute(value, AXIS, along)
            moved = [(sums, "sum")]
        else:
            sums["a"] = lax.ppermute(value[:tok_count], AXIS, along)
            moved = [(sums, "a")]
            if far > 1:
                sums["b"] = lax.ppermute(value[tok_count:], AXIS, across)
                moved.append((sums, "b"))
        if n == 0:
            moved += [(held, ("a", far)), (work, "down")]
            moved += [(others, i) for i in range(len(others))]
            moved += send(hidden_pieces, "hidden", 0, 20)
        elif n == 1:
            moved += send(hidden_pieces, "hidden", 1, 8)
            blocks = [held["ab", i] for i in range(far)] + [held["a", far]]
            blocks += [lax.ppermute(value, AXIS, swap) for value in blocks[1:]]
            work["x"] = gather_rows(
                work["joint"], all_slots, all_slots.astype(jnp.float32), blocks, slot_total, cap, False
            )
            moved.append((work, "x"))
        elif n == 2:
            x = work["x"]
            gate_grads, up_grads = [gate_grad], [up_grad]
            for i in shifts:
                other = pre_grads(
                    whole("hidden", 2, i).astype(jnp.float32), came["saved", 0, i], came["saved", 1, i]
                )
                gate_grads.append(other[0])
                up_grads.append(other[1])
            work["gate"] = over_slots(gate_grads)
            moved += [(work, "gate")] + [(up_grads, i) for i in shifts]
        elif n == 3:
            work["up"] = over_slots(up_grads)
            moved.append((work, "up"))
        if n in (2, 3):
            for i in shifts:
                value = shifted(down_pieces[i - 1][n - 2], i)
                first = work["x"][0, :8, :128] if n == 2 else work["gate"][:8, :128]
                came["down", n - 2, i] = ahead_by(value, 8 if n == 2 else 14, (first,))
                moved.append((came, ("down", n - 2, i)))
        together(*moved)
        if n == 0:
            down_pieces = [split_rows(other, 3) for other in others]

    for i in shifts:
        came["down", 2, i] = ahead_by(shifted(down_pieces[i - 1][2], i), 14, (work["up"][:8, :128],))
    grad_down = work["down"].astype(jnp.float32)
    for i in shifts:
        grad_down = grad_down + whole("down", 3, i).astype(jnp.float32)
    weight = jnp.concatenate([work["gate"], work["up"], grad_down], axis=0)
    trained_flag = jnp.any(trained == me).astype(jnp.float32)
    work["weight"] = (weight * trained_flag).astype(jnp.bfloat16)
    together((work, "weight"), *[(sums, key) for key in ("a", "b") if key in sums])
    in_grad = total(far) + sums["a"].astype(jnp.float32)
    if far > 1:
        in_grad = in_grad + sums["b"].astype(jnp.float32)
    return in_grad.astype(jnp.bfloat16), work["weight"].T[None]


def solution(mesh):
    return jax.shard_map(
        per_device,
        mesh=mesh,
        in_specs=(
            P(("dp", "expert"), None),
            P(("dp", "expert"), None),
            P(("dp", "expert"), None),
            P(("dp", "expert"), None),
            P(),
            P("expert", None, None),
            P("expert", None, None),
            P("dp", "expert", None, None),
        ),
        out_specs=(P(("dp", "expert"), None), P("expert", "dp", None)),
        check_vma=False,
    )
```

```python
import functools

import jax
import jax.numpy as jnp
from jax import lax
from jax.experimental import pallas as pl
from jax.experimental.pallas import tpu as pltpu
from jax.sharding import PartitionSpec as P

AXIS = "expert"
CORES = 2
CONTRACT_LAST = (((1,), (1,)), ((), ()))
CONTRACT_FIRST = (((0,), (0,)), ((), ()))


def chip_cycle(chips):
    width = 1
    while (2 * width) ** 2 <= chips:
        width *= 2
    height = chips // width
    if width == 1:
        return list(range(chips))
    order = [row * width for row in range(height)]
    for back, row in enumerate(reversed(range(height))):
        columns = range(1, width) if back % 2 == 0 else range(width - 1, 0, -1)
        order += [row * width + column for column in columns]
    return order


def after_all(*values):
    return lax.optimization_barrier(values)


def ahead_by(value, microseconds, after=()):
    return pl.pallas_call(
        lambda *refs: None,
        out_shape=jax.ShapeDtypeStruct(value.shape, value.dtype),
        in_specs=[pl.BlockSpec(memory_space=pltpu.HBM)] + [pl.BlockSpec(memory_space=pl.ANY)] * len(after),
        out_specs=pl.BlockSpec(memory_space=pltpu.HBM),
        input_output_aliases={0: 0},
        cost_estimate=pl.CostEstimate(
            flops=0, bytes_accessed=int(microseconds * 3.0e6), transcendentals=0
        ),
        name="ahead_by",
    )(value, *after)


def split_rows(value, count, tile=16):
    tiles = value.shape[0] // tile
    ends = [tile * (tiles * (i + 1) // count) for i in range(count - 1)] + [value.shape[0]]
    return [value[a:b] for a, b in zip([0] + ends[:-1], ends)]


def windows(rows, cap, devices, group):
    span = min(rows, -(-(group * cap + 15) // 16) * 16)
    return [min(d * cap // 16 * 16, rows - span) for d in range(0, devices, group)], span


def gather_kernel(js, slot_ref, gate_ref, *refs, count, planes, cap, group, gated):
    chunks, (out_hbm, buf, out_ref, in_sems, out_sems) = refs[:-5], refs[-5:]
    block = buf.shape[1] // count
    rows, width = out_ref.shape[1], out_ref.shape[2]
    blocks = [
        chunk.at[pl.ds(first, planes * block)]
        for chunk in chunks
        for first in range(0, chunk.shape[0], planes * block)
    ]
    for plane in range(planes):
        for i, source in enumerate(blocks):
            start = pl.multiple_of(js[i] * block, block)
            pltpu.make_async_copy(
                source.at[pl.ds(plane * block, block)],
                buf.at[plane, pl.ds(start, block)],
                in_sems.at[plane, js[i]],
            ).start()
    firsts, span = windows(rows, cap, count, group)
    firsts = firsts + [rows]
    copies = []
    for plane in range(planes):
        done = 0
        for g in range(count // group):
            first = firsts[g]
            for j in range(g * group, (g + 1) * group):
                window = buf.at[plane, pl.ds(j * block, block)]
                pltpu.make_async_copy(window, window, in_sems.at[plane, j]).wait()
            window = slice(g * group * block, (g + 1) * group * block)
            labels = lax.broadcasted_iota(jnp.int32, (span, group * block), 0) + first
            hit = labels == slot_ref[plane : plane + 1, window]
            onehot = hit.astype(jnp.float32).astype(jnp.bfloat16)
            if gated:
                gates = gate_ref[plane : plane + 1, window]
                scale = jnp.sum(jnp.where(hit, gates, 0.0), axis=1, keepdims=True)
            again = max(0, done - first)
            for left in range(0, width, 512):
                lanes = slice(left, left + 512)
                values = jnp.dot(
                    onehot, buf[plane, window, lanes], preferred_element_type=jnp.float32
                )
                if gated:
                    values = values * scale
                values = values.astype(jnp.bfloat16)
                if again:
                    out_ref[plane, first : first + again, lanes] += values[:again]
                if again < span:
                    out_ref[plane, first + again : first + span, lanes] = values[again:]
            done = first + span
            place = pl.ds(first, firsts[g + 1] - first)
            copy = pltpu.make_async_copy(
                out_ref.at[plane, place], out_hbm.at[plane, place], out_sems.at[plane, g]
            )
            copy.start()
            copies.append(copy)
    for copy in copies:
        copy.wait()


def gather_rows(js, slots, gates, chunks, rows, cap, gated):
    planes, count, group = slots.shape[0], js.shape[0], CORES
    block, width = slots.shape[1] // count, chunks[0].shape[1]
    return pl.pallas_call(
        functools.partial(
            gather_kernel, count=count, planes=planes, cap=cap, group=group, gated=gated
        ),
        out_shape=jax.ShapeDtypeStruct((planes, rows, width), jnp.bfloat16),
        grid_spec=pltpu.PrefetchScalarGridSpec(
            num_scalar_prefetch=1,
            grid=(1,),
            in_specs=[pl.BlockSpec(slots.shape, lambda i, js: (0, 0))] * 2
            + [pl.BlockSpec(memory_space=pl.ANY)] * len(chunks),
            out_specs=pl.BlockSpec(memory_space=pltpu.HBM),
            scratch_shapes=[
                pltpu.VMEM((planes, count * block, width), jnp.bfloat16),
                pltpu.VMEM((planes, rows, width), jnp.bfloat16),
                pltpu.SemaphoreType.DMA((planes, count)),
                pltpu.SemaphoreType.DMA((planes, count // group)),
            ],
        ),
        compiler_params=pltpu.CompilerParams(vmem_limit_bytes=58 * 2**20),
        cost_estimate=pl.CostEstimate(
            flops=0,
            bytes_accessed=int(2 * planes * (count * block + rows) * width * 2),
            transcendentals=0,
        ),
        name="gather_rows",
    )(js, slots, gates, *chunks)


def scatter_kernel(js, slot_ref, grad_ref, *refs, sizes, cap, span):
    outs, buf, sems = refs[:-2], refs[-2], refs[-1]
    count, block, width = buf.shape
    rows = grad_ref.shape[0]
    listed = count // CORES
    copies = []
    places = [(n, at) for n, size in enumerate(sizes) for at in range(size)]
    for order in range(count):
        x, side = order // CORES, order % CORES
        i, (n, at) = x + side * listed, places[x]
        j = js[i]
        first = pl.multiple_of(jnp.minimum(j * cap // 16 * 16, rows - span), 16)
        slots = slot_ref[pl.ds(j, 1), :]
        labels = lax.broadcasted_iota(jnp.int32, (span, block), 0) + first
        onehot = (labels == slots).astype(jnp.float32).astype(jnp.bfloat16)
        for left in range(0, width, 512):
            values = lax.dot_general(
                onehot,
                grad_ref[pl.ds(first, span), left : left + 512],
                CONTRACT_FIRST,
                preferred_element_type=jnp.float32,
            )
            buf[i, :, left : left + 512] = values.astype(jnp.bfloat16)
        out = outs[n + side * len(sizes)].at[pl.ds(at * block, block)]
        copies.append(pltpu.make_async_copy(buf.at[i], out, sems.at[i]))
        copies[-1].start()
    for copy in copies:
        copy.wait()


def scatter_rows(js, slots, grads, cap, sizes):
    count, block = slots.shape
    rows, width = grads.shape
    span = min(rows, -(-(cap + 15) // 16) * 16)
    return pl.pallas_call(
        functools.partial(scatter_kernel, sizes=sizes, cap=cap, span=span),
        out_shape=[jax.ShapeDtypeStruct((n * block, width), jnp.bfloat16) for n in sizes] * CORES,
        grid_spec=pltpu.PrefetchScalarGridSpec(
            num_scalar_prefetch=1,
            grid=(1,),
            in_specs=[
                pl.BlockSpec(slots.shape, lambda i, js: (0, 0)),
                pl.BlockSpec(grads.shape, lambda i, js: (0, 0)),
            ],
            out_specs=[pl.BlockSpec(memory_space=pltpu.HBM)] * (CORES * len(sizes)),
            scratch_shapes=[
                pltpu.VMEM((count, block, width), jnp.bfloat16),
                pltpu.SemaphoreType.DMA((count,)),
            ],
        ),
        compiler_params=pltpu.CompilerParams(vmem_limit_bytes=58 * 2**20),
        cost_estimate=pl.CostEstimate(
            flops=2 * count * span * block * width,
            bytes_accessed=int(2 * (rows + count * block) * width * 2),
            transcendentals=0,
        ),
        name="scatter_rows",
    )(js, slots, grads)


def per_device(tokens, out_grad, expert_ids, gate_weights, trained, w_in, w_down, saved):
    groups, replicas = lax.axis_size(AXIS), lax.axis_size("dp")
    chips = groups // CORES
    tok_count, model_width = tokens.shape
    slot_total = saved.shape[2]
    cap = slot_total // groups
    hidden_units = w_down.shape[1]
    cut = model_width // replicas
    me, replica = lax.axis_index(AXIS), lax.axis_index("dp")
    shifts = range(1, replicas)

    far = chips // 2
    order = chip_cycle(chips)
    place = {c: i for i, c in enumerate(order)}

    def at(device, steps):
        return order[(place[device // CORES] + (steps if device % CORES == 0 else -steps)) % chips]

    along = [(i, CORES * at(i, 1) + i % CORES) for i in range(groups)]
    across = [(i, CORES * at(i, 1) + 1 - i % CORES) for i in range(groups)]
    swap = [(i, i ^ 1) for i in range(groups)]
    names = [("a", 0), ("b", 0)]
    names += [(kind, i) for i in range(1, far + 1) for kind in "ab" if (kind, i) != ("b", far)]
    pairs = names[:1] + names[2:]

    def device_at(device, name, way):
        kind, steps = name
        return CORES * at(device, way * steps) + (device % CORES if kind == "a" else 1 - device % CORES)

    def listing(own, other, way):
        table = [
            [device_at(i, name, way) for name in own] + [device_at(i ^ 1, name, way) for name in other]
            for i in range(groups)
        ]
        size = len(own) + len(other)
        return lax.dynamic_slice(jnp.array(table, jnp.int32), (me, 0), (1, size))[0]

    leaving = [("a", far)] + [(kind, i) for i in range(far - 1, 0, -1) for kind in "ab"] + [("a", 0)]
    sizes = [1] + [2] * (far - 1) + [1]
    work = {
        "js": listing(pairs, pairs, -1),
        "joint": listing(names, names[2:], -1),
        "leaving": listing(leaving, leaving, 1),
    }

    def shifted(value, shift):
        return lax.ppermute(value, "dp", [(r, (r + shift) % replicas) for r in range(replicas)])

    def columns(value, owner):
        return lax.dynamic_slice_in_dim(value, owner * cut, cut, 1)

    def together(*places):
        values = after_all(*[box[key] for box, key in places])
        for (box, key), value in zip(places, values):
            box[key] = value

    came = {}

    def send(pieces, label, i, early):
        for shift in shifts:
            value = shifted(pieces[i], shift)
            came[label, i, shift] = ahead_by(value, early) if early else value
        return [(came, (label, i, shift)) for shift in shifts]

    def whole(label, count, shift):
        return jnp.concatenate([came[label, i, shift] for i in range(count)], axis=0)

    def hop(blocks, kind, step):
        blocks[kind, step] = lax.ppermute(blocks[kind, step - 1], AXIS, along)
        return blocks, (kind, step)

    def exchange(blocks, name):
        blocks["other", name] = lax.ppermute(blocks[name], AXIS, swap)
        return blocks, ("other", name)

    def all_blocks(blocks):
        return [blocks[name] for name in pairs] + [blocks["other", name] for name in pairs]

    labels = jnp.arange(groups, dtype=jnp.int32)
    chosen = expert_ids[None, :, :] == labels[:, None, None]
    routed = jnp.any(chosen, axis=2)
    gate = jnp.sum(jnp.where(chosen, gate_weights[None], 0.0), axis=2)
    earlier = jnp.triu(jnp.ones((tok_count, tok_count), jnp.bfloat16), 1)
    rank = jnp.dot(routed.astype(jnp.bfloat16), earlier, preferred_element_type=jnp.float32)
    slot = jnp.where(routed, rank + (me * cap).astype(jnp.float32), -1.0)
    listed = [gate, slot] + [shifted(slot, i) for i in shifts]
    halves = [columns(tokens, (replica + i) % replicas) for i in range(replicas)]
    work["halves"] = jnp.concatenate(
        [halves[0]] + [shifted(halves[i], i) for i in shifts], axis=0
    )
    own_rows = saved.reshape(slot_total, 2 * hidden_units)
    gate_pre, up_pre = own_rows[:, :hidden_units], own_rows[:, hidden_units:]
    work["saved"] = own_rows

    grads = {("a", 0): out_grad}
    grads["b", 0] = exchange(grads, ("a", 0))[0]["other", ("a", 0)]
    for step in range(1, far + 1):
        moved = [hop(grads, "a", step)]
        if step < far:
            hop(grads, "b", step)
        if step == 1:
            together((grads, ("b", 1)), (listed, -1), (work, "halves"), (work, "saved"))
        elif step == 2:
            places = [(work, key) for key in ("js", "joint", "leaving", "saved")]
            together((grads, ("a", 2)), *places)
        elif step == 3:
            moved += [exchange(grads, (kind, 1)) for kind in "ab"] + [(saved_pieces, 1)]
        elif step == far:
            moved += [exchange(grads, (kind, 2)) for kind in "ab"]
            work["gates"] = work["info"][:, 0, :].reshape(1, -1)
            all_slots = jnp.swapaxes(work["info"][:, 1:, :], 0, 1).astype(jnp.int32)
            work["slots"] = all_slots.reshape(replicas, -1)
            work["own"] = all_slots[0]
            moved += [(work, key) for key in ("gates", "slots", "own")]
        together(*moved)
        if step == 2:
            saved_pieces[1] = work["saved"][:, hidden_units:]
        if step == 1:
            saved_pieces = [work["saved"][:, :hidden_units], None]
            work["info"] = lax.all_to_all(
                jnp.stack(listed, axis=1), AXIS, split_axis=0, concat_axis=0, tiled=True
            )
        elif step == far - 1:
            together((work, "info"), (grads, ("b", step)))
    held = {("a", 0): work["halves"]}
    exchange(held, ("a", 0))
    held["ab", 0] = jnp.concatenate([held["a", 0], held["other", ("a", 0)]], axis=0)
    together((held, ("ab", 0)), (grads, ("b", far - 1)), *send(saved_pieces, "saved", 0, 18))
    grads["a", far] = ahead_by(grads["a", far], 14)
    for name in pairs:
        if ("other", name) not in grads:
            exchange(grads, name)
    hop(held, "ab", 1)
    js, gates, all_slots = work["js"], work["gates"], work["slots"]

    def pre_grads(hidden_grad, gate_pre, up_pre):
        gate_pre, up_pre = gate_pre.astype(jnp.float32), up_pre.astype(jnp.float32)
        sigmoid_gate = jax.nn.sigmoid(gate_pre)
        activated = gate_pre * sigmoid_gate
        gate_grad = hidden_grad * up_pre * sigmoid_gate * (1.0 + gate_pre * (1.0 - sigmoid_gate))
        up_grad = hidden_grad * activated
        hidden = activated * up_pre
        return [value.astype(jnp.bfloat16) for value in (gate_grad, up_grad, hidden)]

    def down_part(owner):
        return lax.dot_general(
            hidden, columns(s, owner), CONTRACT_FIRST, preferred_element_type=jnp.float32
        )

    work["s"] = gather_rows(js, all_slots[:1], gates, all_blocks(grads), slot_total, cap, True)[0]
    together((work, "s"), (held, ("ab", 1)))
    s = work["s"]
    hidden_grad = lax.dot_general(s, w_down[0], CONTRACT_LAST, preferred_element_type=jnp.float32)
    gate_grad, up_grad, hidden = pre_grads(hidden_grad, gate_pre, up_pre)
    hidden_pieces = split_rows(hidden_grad.astype(jnp.bfloat16), 2, 8)
    work["slot_grads"] = lax.dot_general(
        jnp.concatenate([gate_grad, up_grad], axis=1), w_in[0], CONTRACT_LAST, preferred_element_type=jnp.float32
    ).astype(jnp.bfloat16)
    moved = [hop(held, "ab", 2)]
    together((work, "slot_grads"), *moved)
    parts = scatter_rows(work["leaving"], work["own"], work["slot_grads"], cap, sizes)
    for i in range(len(parts)):
        work["part", i] = parts[i]
    moved = [(work, ("part", i)) for i in range(len(parts))] + send(saved_pieces, "saved", 1, 14)
    together(*moved, hop(held, "ab", 3))
    parts = [work["part", i] for i in range(len(parts))]
    for step in range(4, far):
        hop(held, "ab", step)
    held["a", far] = lax.ppermute(
        lax.slice_in_dim(held["ab", far - 1], 0, replicas * tok_count), AXIS, along
    )
    kept, sent = parts[: len(sizes)], parts[len(sizes) :]
    others = [down_part((replica + i) % replicas).astype(jnp.bfloat16) for i in shifts]
    work["down"] = down_part(replica).astype(jnp.bfloat16)
    swapped = [lax.ppermute(value, AXIS, swap) for value in sent]

    def total(n):
        return kept[n].astype(jnp.float32) + swapped[n].astype(jnp.float32)

    def over_slots(values):
        return sum(
            lax.dot_general(values[i], x[i], CONTRACT_FIRST, preferred_element_type=jnp.float32)
            for i in range(replicas)
        )

    sums = {}
    for n in range(far):
        value = total(n)
        if n == 1:
            value = value + jnp.pad(sums["sum"].astype(jnp.float32), ((0, tok_count), (0, 0)))
        elif n:
            value = value + sums["sum"].astype(jnp.float32)
        value = value.astype(jnp.bfloat16)
        if n < far - 1:
            sums["sum"] = lax.ppermute(value, AXIS, along)
            moved = [(sums, "sum")]
        else:
            sums["a"] = lax.ppermute(value[:tok_count], AXIS, along)
            moved = [(sums, "a")]
            if far > 1:
                sums["b"] = lax.ppermute(value[tok_count:], AXIS, across)
                moved.append((sums, "b"))
        if n == 0:
            moved += [(held, ("a", far)), (work, "down")]
            moved += [(others, i) for i in range(len(others))]
            moved += send(hidden_pieces, "hidden", 0, 20)
        elif n == 1:
            moved += send(hidden_pieces, "hidden", 1, 8)
            blocks = [held["ab", i] for i in range(far)] + [held["a", far]]
            blocks += [lax.ppermute(value, AXIS, swap) for value in blocks[1:]]
            work["x"] = gather_rows(
                work["joint"], all_slots, all_slots.astype(jnp.float32), blocks, slot_total, cap, False
            )
            moved.append((work, "x"))
        elif n == 2:
            x = work["x"]
            gate_grads, up_grads = [gate_grad], [up_grad]
            for i in shifts:
                other = pre_grads(
                    whole("hidden", 2, i).astype(jnp.float32), came["saved", 0, i], came["saved", 1, i]
                )
                gate_grads.append(other[0])
                up_grads.append(other[1])
            work["gate"] = over_slots(gate_grads)
            moved += [(work, "gate")] + [(up_grads, i) for i in shifts]
        elif n == 3:
            work["up"] = over_slots(up_grads)
            moved.append((work, "up"))
        if n in (2, 3):
            for i in shifts:
                value = shifted(down_pieces[i - 1][n - 2], i)
                first = work["x"][0, :8, :128] if n == 2 else work["gate"][:8, :128]
                came["down", n - 2, i] = ahead_by(value, 8 if n == 2 else 14, (first,))
                moved.append((came, ("down", n - 2, i)))
        together(*moved)
        if n == 0:
            down_pieces = [split_rows(other, 3) for other in others]

    for i in shifts:
        came["down", 2, i] = ahead_by(shifted(down_pieces[i - 1][2], i), 14, (work["up"][:8, :128],))
    grad_down = work["down"].astype(jnp.float32)
    for i in shifts:
        grad_down = grad_down + whole("down", 3, i).astype(jnp.float32)
    weight = jnp.concatenate([work["gate"], work["up"], grad_down], axis=0)
    trained_flag = jnp.any(trained == me).astype(jnp.float32)
    work["weight"] = (weight * trained_flag).astype(jnp.bfloat16)
    together((work, "weight"), *[(sums, key) for key in ("a", "b") if key in sums])
    in_grad = total(far) + sums["a"].astype(jnp.float32)
    if far > 1:
        in_grad = in_grad + sums["b"].astype(jnp.float32)
    return in_grad.astype(jnp.bfloat16), work["weight"].T[None]


def solution(mesh):
    return jax.shard_map(
        per_device,
        mesh=mesh,
        in_specs=(
            P(("dp", "expert"), None),
            P(("dp", "expert"), None),
            P(("dp", "expert"), None),
            P(("dp", "expert"), None),
            P(),
            P("expert", None, None),
            P("expert", None, None),
            P("dp", "expert", None, None),
        ),
        out_specs=(P(("dp", "expert"), None), P("expert", "dp", None)),
        check_vma=False,
    )
```

```python
import functools

import jax
import jax.numpy as jnp
from jax import lax
from jax.experimental import pallas as pl
from jax.experimental.pallas import tpu as pltpu
from jax.sharding import PartitionSpec as P

AXIS = "expert"
CORES = 2
CONTRACT_LAST = (((1,), (1,)), ((), ()))
CONTRACT_FIRST = (((0,), (0,)), ((), ()))


def chip_cycle(chips):
    width = 1
    while (2 * width) ** 2 <= chips:
        width *= 2
    height = chips // width
    if width == 1:
        return list(range(chips))
    order = [row * width for row in range(height)]
    for back, row in enumerate(reversed(range(height))):
        columns = range(1, width) if back % 2 == 0 else range(width - 1, 0, -1)
        order += [row * width + column for column in columns]
    return order


def after_all(*values):
    return lax.optimization_barrier(values)


def ahead_by(value, microseconds, after=()):
    return pl.pallas_call(
        lambda *refs: None,
        out_shape=jax.ShapeDtypeStruct(value.shape, value.dtype),
        in_specs=[pl.BlockSpec(memory_space=pltpu.HBM)] + [pl.BlockSpec(memory_space=pl.ANY)] * len(after),
        out_specs=pl.BlockSpec(memory_space=pltpu.HBM),
        input_output_aliases={0: 0},
        cost_estimate=pl.CostEstimate(
            flops=0, bytes_accessed=int(microseconds * 3.0e6), transcendentals=0
        ),
        name="ahead_by",
    )(value, *after)


def split_rows(value, count, tile=16):
    tiles = value.shape[0] // tile
    ends = [tile * (tiles * (i + 1) // count) for i in range(count - 1)] + [value.shape[0]]
    return [value[a:b] for a, b in zip([0] + ends[:-1], ends)]


def windows(rows, cap, devices, group):
    span = min(rows, -(-(group * cap + 15) // 16) * 16)
    return [min(d * cap // 16 * 16, rows - span) for d in range(0, devices, group)], span


def gather_kernel(js, slot_ref, gate_ref, *refs, count, planes, cap, group, gated):
    chunks, (out_hbm, buf, out_ref, in_sems, out_sems) = refs[:-5], refs[-5:]
    block = buf.shape[1] // count
    rows, width = out_ref.shape[1], out_ref.shape[2]
    blocks = [
        chunk.at[pl.ds(first, planes * block)]
        for chunk in chunks
        for first in range(0, chunk.shape[0], planes * block)
    ]
    for plane in range(planes):
        for i, source in enumerate(blocks):
            start = pl.multiple_of(js[i] * block, block)
            pltpu.make_async_copy(
                source.at[pl.ds(plane * block, block)],
                buf.at[plane, pl.ds(start, block)],
                in_sems.at[plane, js[i]],
            ).start()
    firsts, span = windows(rows, cap, count, group)
    firsts = firsts + [rows]
    copies = []
    for plane in range(planes):
        done = 0
        for g in range(count // group):
            first = firsts[g]
            for j in range(g * group, (g + 1) * group):
                window = buf.at[plane, pl.ds(j * block, block)]
                pltpu.make_async_copy(window, window, in_sems.at[plane, j]).wait()
            window = slice(g * group * block, (g + 1) * group * block)
            labels = lax.broadcasted_iota(jnp.int32, (span, group * block), 0) + first
            hit = labels == slot_ref[plane : plane + 1, window]
            onehot = hit.astype(jnp.float32).astype(jnp.bfloat16)
            if gated:
                gates = gate_ref[plane : plane + 1, window]
                scale = jnp.sum(jnp.where(hit, gates, 0.0), axis=1, keepdims=True)
            again = max(0, done - first)
            for left in range(0, width, 512):
                lanes = slice(left, left + 512)
                values = jnp.dot(
                    onehot, buf[plane, window, lanes], preferred_element_type=jnp.float32
                )
                if gated:
                    values = values * scale
                values = values.astype(jnp.bfloat16)
                if again:
                    out_ref[plane, first : first + again, lanes] += values[:again]
                if again < span:
                    out_ref[plane, first + again : first + span, lanes] = values[again:]
            done = first + span
            place = pl.ds(first, firsts[g + 1] - first)
            copy = pltpu.make_async_copy(
                out_ref.at[plane, place], out_hbm.at[plane, place], out_sems.at[plane, g]
            )
            copy.start()
            copies.append(copy)
    for copy in copies:
        copy.wait()


def gather_rows(js, slots, gates, chunks, rows, cap, gated):
    planes, count, group = slots.shape[0], js.shape[0], CORES
    block, width = slots.shape[1] // count, chunks[0].shape[1]
    return pl.pallas_call(
        functools.partial(
            gather_kernel, count=count, planes=planes, cap=cap, group=group, gated=gated
        ),
        out_shape=jax.ShapeDtypeStruct((planes, rows, width), jnp.bfloat16),
        grid_spec=pltpu.PrefetchScalarGridSpec(
            num_scalar_prefetch=1,
            grid=(1,),
            in_specs=[pl.BlockSpec(slots.shape, lambda i, js: (0, 0))] * 2
            + [pl.BlockSpec(memory_space=pl.ANY)] * len(chunks),
            out_specs=pl.BlockSpec(memory_space=pltpu.HBM),
            scratch_shapes=[
                pltpu.VMEM((planes, count * block, width), jnp.bfloat16),
                pltpu.VMEM((planes, rows, width), jnp.bfloat16),
                pltpu.SemaphoreType.DMA((planes, count)),
                pltpu.SemaphoreType.DMA((planes, count // group)),
            ],
        ),
        compiler_params=pltpu.CompilerParams(vmem_limit_bytes=58 * 2**20),
        cost_estimate=pl.CostEstimate(
            flops=0,
            bytes_accessed=int(2 * planes * (count * block + rows) * width * 2),
            transcendentals=0,
        ),
        name="gather_rows",
    )(js, slots, gates, *chunks)


def scatter_kernel(js, slot_ref, grad_ref, *refs, sizes, cap, span):
    outs, buf, sems = refs[:-2], refs[-2], refs[-1]
    count, block, width = buf.shape
    rows = grad_ref.shape[0]
    listed = count // CORES
    copies = []
    places = [(n, at) for n, size in enumerate(sizes) for at in range(size)]
    for order in range(count):
        x, side = order // CORES, order % CORES
        i, (n, at) = x + side * listed, places[x]
        j = js[i]
        first = pl.multiple_of(jnp.minimum(j * cap // 16 * 16, rows - span), 16)
        slots = slot_ref[pl.ds(j, 1), :]
        labels = lax.broadcasted_iota(jnp.int32, (span, block), 0) + first
        onehot = (labels == slots).astype(jnp.float32).astype(jnp.bfloat16)
        for left in range(0, width, 512):
            values = lax.dot_general(
                onehot,
                grad_ref[pl.ds(first, span), left : left + 512],
                CONTRACT_FIRST,
                preferred_element_type=jnp.float32,
            )
            buf[i, :, left : left + 512] = values.astype(jnp.bfloat16)
        out = outs[n + side * len(sizes)].at[pl.ds(at * block, block)]
        copies.append(pltpu.make_async_copy(buf.at[i], out, sems.at[i]))
        copies[-1].start()
    for copy in copies:
        copy.wait()


def scatter_rows(js, slots, grads, cap, sizes):
    count, block = slots.shape
    rows, width = grads.shape
    span = min(rows, -(-(cap + 15) // 16) * 16)
    return pl.pallas_call(
        functools.partial(scatter_kernel, sizes=sizes, cap=cap, span=span),
        out_shape=[jax.ShapeDtypeStruct((n * block, width), jnp.bfloat16) for n in sizes] * CORES,
        grid_spec=pltpu.PrefetchScalarGridSpec(
            num_scalar_prefetch=1,
            grid=(1,),
            in_specs=[
                pl.BlockSpec(slots.shape, lambda i, js: (0, 0)),
                pl.BlockSpec(grads.shape, lambda i, js: (0, 0)),
            ],
            out_specs=[pl.BlockSpec(memory_space=pltpu.HBM)] * (CORES * len(sizes)),
            scratch_shapes=[
                pltpu.VMEM((count, block, width), jnp.bfloat16),
                pltpu.SemaphoreType.DMA((count,)),
            ],
        ),
        compiler_params=pltpu.CompilerParams(vmem_limit_bytes=58 * 2**20),
        cost_estimate=pl.CostEstimate(
            flops=2 * count * span * block * width,
            bytes_accessed=int(2 * (rows + count * block) * width * 2),
            transcendentals=0,
        ),
        name="scatter_rows",
    )(js, slots, grads)


def per_device(tokens, out_grad, expert_ids, gate_weights, trained, w_in, w_down, saved):
    groups, replicas = lax.axis_size(AXIS), lax.axis_size("dp")
    chips = groups // CORES
    tok_count, model_width = tokens.shape
    slot_total = saved.shape[2]
    cap = slot_total // groups
    hidden_units = w_down.shape[1]
    cut = model_width // replicas
    me, replica = lax.axis_index(AXIS), lax.axis_index("dp")
    shifts = range(1, replicas)

    far = chips // 2
    order = chip_cycle(chips)
    place = {c: i for i, c in enumerate(order)}

    def at(device, steps):
        return order[(place[device // CORES] + (steps if device % CORES == 0 else -steps)) % chips]

    along = [(i, CORES * at(i, 1) + i % CORES) for i in range(groups)]
    across = [(i, CORES * at(i, 1) + 1 - i % CORES) for i in range(groups)]
    swap = [(i, i ^ 1) for i in range(groups)]
    names = [("a", 0), ("b", 0)]
    names += [(kind, i) for i in range(1, far + 1) for kind in "ab" if (kind, i) != ("b", far)]
    pairs = names[:1] + names[2:]

    def device_at(device, name, way):
        kind, steps = name
        return CORES * at(device, way * steps) + (device % CORES if kind == "a" else 1 - device % CORES)

    def listing(own, other, way):
        table = [
            [device_at(i, name, way) for name in own] + [device_at(i ^ 1, name, way) for name in other]
            for i in range(groups)
        ]
        size = len(own) + len(other)
        return lax.dynamic_slice(jnp.array(table, jnp.int32), (me, 0), (1, size))[0]

    leaving = [("a", far)] + [(kind, i) for i in range(far - 1, 0, -1) for kind in "ab"] + [("a", 0)]
    sizes = [1] + [2] * (far - 1) + [1]
    work = {
        "js": listing(pairs, pairs, -1),
        "joint": listing(names, names[2:], -1),
        "leaving": listing(leaving, leaving, 1),
    }

    def shifted(value, shift):
        return lax.ppermute(value, "dp", [(r, (r + shift) % replicas) for r in range(replicas)])

    def columns(value, owner):
        return lax.dynamic_slice_in_dim(value, owner * cut, cut, 1)

    def together(*places):
        values = after_all(*[box[key] for box, key in places])
        for (box, key), value in zip(places, values):
            box[key] = value

    came = {}

    def send(pieces, label, i, early):
        for shift in shifts:
            value = shifted(pieces[i], shift)
            came[label, i, shift] = ahead_by(value, early) if early else value
        return [(came, (label, i, shift)) for shift in shifts]

    def whole(label, count, shift):
        return jnp.concatenate([came[label, i, shift] for i in range(count)], axis=0)

    def hop(blocks, kind, step):
        blocks[kind, step] = lax.ppermute(blocks[kind, step - 1], AXIS, along)
        return blocks, (kind, step)

    def exchange(blocks, name):
        blocks["other", name] = lax.ppermute(blocks[name], AXIS, swap)
        return blocks, ("other", name)

    def all_blocks(blocks):
        return [blocks[name] for name in pairs] + [blocks["other", name] for name in pairs]

    labels = jnp.arange(groups, dtype=jnp.int32)
    chosen = expert_ids[None, :, :] == labels[:, None, None]
    routed = jnp.any(chosen, axis=2)
    gate = jnp.sum(jnp.where(chosen, gate_weights[None], 0.0), axis=2)
    earlier = jnp.triu(jnp.ones((tok_count, tok_count), jnp.bfloat16), 1)
    rank = jnp.dot(routed.astype(jnp.bfloat16), earlier, preferred_element_type=jnp.float32)
    slot = jnp.where(routed, rank + (me * cap).astype(jnp.float32), -1.0)
    listed = [gate, slot] + [shifted(slot, i) for i in shifts]
    halves = [columns(tokens, (replica + i) % replicas) for i in range(replicas)]
    work["halves"] = jnp.concatenate(
        [halves[0]] + [shifted(halves[i], i) for i in shifts], axis=0
    )
    own_rows = saved.reshape(slot_total, 2 * hidden_units)
    gate_pre, up_pre = own_rows[:, :hidden_units], own_rows[:, hidden_units:]
    work["saved"] = own_rows

    grads = {("a", 0): out_grad}
    grads["b", 0] = exchange(grads, ("a", 0))[0]["other", ("a", 0)]
    for step in range(1, far + 1):
        moved = [hop(grads, "a", step)]
        if step < far:
            hop(grads, "b", step)
        if step == 1:
            together((grads, ("b", 1)), (listed, -1), (work, "halves"), (work, "saved"))
        elif step == 2:
            places = [(work, key) for key in ("js", "joint", "leaving", "saved")]
            together((grads, ("a", 2)), *places)
        elif step == 3:
            moved += [exchange(grads, (kind, 1)) for kind in "ab"] + [(saved_pieces, 1)]
        elif step == far:
            moved += [exchange(grads, (kind, 2)) for kind in "ab"]
            work["gates"] = work["info"][:, 0, :].reshape(1, -1)
            all_slots = jnp.swapaxes(work["info"][:, 1:, :], 0, 1).astype(jnp.int32)
            work["slots"] = all_slots.reshape(replicas, -1)
            work["own"] = all_slots[0]
            moved += [(work, key) for key in ("gates", "slots", "own")]
        together(*moved)
        if step == 2:
            saved_pieces[1] = work["saved"][:, hidden_units:]
        if step == 1:
            saved_pieces = [work["saved"][:, :hidden_units], None]
            work["info"] = lax.all_to_all(
                jnp.stack(listed, axis=1), AXIS, split_axis=0, concat_axis=0, tiled=True
            )
        elif step == far - 1:
            together((work, "info"), (grads, ("b", step)))
    held = {("a", 0): work["halves"]}
    exchange(held, ("a", 0))
    held["ab", 0] = jnp.concatenate([held["a", 0], held["other", ("a", 0)]], axis=0)
    together((held, ("ab", 0)), (grads, ("b", far - 1)), *send(saved_pieces, "saved", 0, 18))
    grads["a", far] = ahead_by(grads["a", far], 14)
    for name in pairs:
        if ("other", name) not in grads:
            exchange(grads, name)
    hop(held, "ab", 1)
    js, gates, all_slots = work["js"], work["gates"], work["slots"]

    def pre_grads(hidden_grad, gate_pre, up_pre):
        gate_pre, up_pre = gate_pre.astype(jnp.float32), up_pre.astype(jnp.float32)
        sigmoid_gate = jax.nn.sigmoid(gate_pre)
        activated = gate_pre * sigmoid_gate
        gate_grad = hidden_grad * up_pre * sigmoid_gate * (1.0 + gate_pre * (1.0 - sigmoid_gate))
        up_grad = hidden_grad * activated
        hidden = activated * up_pre
        return [value.astype(jnp.bfloat16) for value in (gate_grad, up_grad, hidden)]

    def down_part(owner):
        return lax.dot_general(
            hidden, columns(s, owner), CONTRACT_FIRST, preferred_element_type=jnp.float32
        )

    work["s"] = gather_rows(js, all_slots[:1], gates, all_blocks(grads), slot_total, cap, True)[0]
    together((work, "s"), (held, ("ab", 1)))
    s = work["s"]
    hidden_grad = lax.dot_general(s, w_down[0], CONTRACT_LAST, preferred_element_type=jnp.float32)
    gate_grad, up_grad, hidden = pre_grads(hidden_grad, gate_pre, up_pre)
    hidden_pieces = split_rows(hidden_grad.astype(jnp.bfloat16), 2, 8)
    work["slot_grads"] = lax.dot_general(
        jnp.concatenate([gate_grad, up_grad], axis=1), w_in[0], CONTRACT_LAST, preferred_element_type=jnp.float32
    ).astype(jnp.bfloat16)
    moved = [hop(held, "ab", 2)]
    together((work, "slot_grads"), *moved)
    parts = scatter_rows(work["leaving"], work["own"], work["slot_grads"], cap, sizes)
    for i in range(len(parts)):
        work["part", i] = parts[i]
    moved = [(work, ("part", i)) for i in range(len(parts))] + send(saved_pieces, "saved", 1, 14)
    together(*moved, hop(held, "ab", 3))
    parts = [work["part", i] for i in range(len(parts))]
    for step in range(4, far):
        hop(held, "ab", step)
    held["a", far] = lax.ppermute(
        lax.slice_in_dim(held["ab", far - 1], 0, replicas * tok_count), AXIS, along
    )
    kept, sent = parts[: len(sizes)], parts[len(sizes) :]
    others = [down_part((replica + i) % replicas).astype(jnp.bfloat16) for i in shifts]
    work["down"] = down_part(replica).astype(jnp.bfloat16)
    swapped = [lax.ppermute(value, AXIS, swap) for value in sent]

    def total(n):
        return kept[n].astype(jnp.float32) + swapped[n].astype(jnp.float32)

    def over_slots(values):
        return sum(
            lax.dot_general(values[i], x[i], CONTRACT_FIRST, preferred_element_type=jnp.float32)
            for i in range(replicas)
        )

    sums = {}
    for n in range(far):
        value = total(n)
        if n == 1:
            value = value + jnp.pad(sums["sum"].astype(jnp.float32), ((0, tok_count), (0, 0)))
        elif n:
            value = value + sums["sum"].astype(jnp.float32)
        value = value.astype(jnp.bfloat16)
        if n < far - 1:
            sums["sum"] = lax.ppermute(value, AXIS, along)
            moved = [(sums, "sum")]
        else:
            terms = [kept[n], swapped[n]] + [sums["sum"]] * (n > 1)
            last = []
            for half in (slice(0, tok_count), slice(tok_count, None)):
                rows = [term[half].astype(jnp.float32) for term in terms]
                last.append(sum(rows[1:], rows[0]).astype(jnp.bfloat16))
            sums["a"] = lax.ppermute(last[0] if n > 1 else value[:tok_count], AXIS, along)
            moved = [(sums, "a")]
            if far > 1:
                sums["b"] = lax.ppermute(last[1] if n > 1 else value[tok_count:], AXIS, across)
                moved.append((sums, "b"))
        if n == 0:
            moved += [(held, ("a", far)), (work, "down")]
            moved += [(others, i) for i in range(len(others))]
            moved += send(hidden_pieces, "hidden", 0, 20)
        elif n == 1:
            moved += send(hidden_pieces, "hidden", 1, 8)
            blocks = [held["ab", i] for i in range(far)] + [held["a", far]]
            blocks += [lax.ppermute(value, AXIS, swap) for value in blocks[1:]]
            work["x"] = gather_rows(
                work["joint"], all_slots, all_slots.astype(jnp.float32), blocks, slot_total, cap, False
            )
            moved.append((work, "x"))
        elif n == 2:
            x = work["x"]
            gate_grads, up_grads = [gate_grad], [up_grad]
            for i in shifts:
                other = pre_grads(
                    whole("hidden", 2, i).astype(jnp.float32), came["saved", 0, i], came["saved", 1, i]
                )
                gate_grads.append(other[0])
                up_grads.append(other[1])
            work["gate"] = over_slots(gate_grads)
            moved += [(work, "gate")] + [(up_grads, i) for i in shifts]
        elif n == 3:
            work["up"] = over_slots(up_grads)
            moved.append((work, "up"))
        if n in (2, 3):
            for i in shifts:
                value = shifted(down_pieces[i - 1][n - 2], i)
                first = work["x"][0, :8, :128] if n == 2 else work["gate"][:8, :128]
                came["down", n - 2, i] = ahead_by(value, 8 if n == 2 else 14, (first,))
                moved.append((came, ("down", n - 2, i)))
        together(*moved)
        if n == 0:
            down_pieces = [split_rows(other, 3) for other in others]

    for i in shifts:
        came["down", 2, i] = ahead_by(shifted(down_pieces[i - 1][2], i), 14, (work["up"][:8, :128],))
    grad_down = work["down"].astype(jnp.float32)
    for i in shifts:
        grad_down = grad_down + whole("down", 3, i).astype(jnp.float32)
    weight = jnp.concatenate([work["gate"], work["up"], grad_down], axis=0)
    trained_flag = jnp.any(trained == me).astype(jnp.float32)
    work["weight"] = (weight * trained_flag).astype(jnp.bfloat16)
    together((work, "weight"), *[(sums, key) for key in ("a", "b") if key in sums])
    in_grad = total(far) + sums["a"].astype(jnp.float32)
    if far > 1:
        in_grad = in_grad + sums["b"].astype(jnp.float32)
    return in_grad.astype(jnp.bfloat16), work["weight"].T[None]


def solution(mesh):
    return jax.shard_map(
        per_device,
        mesh=mesh,
        in_specs=(
            P(("dp", "expert"), None),
            P(("dp", "expert"), None),
            P(("dp", "expert"), None),
            P(("dp", "expert"), None),
            P(),
            P("expert", None, None),
            P("expert", None, None),
            P("dp", "expert", None, None),
        ),
        out_specs=(P(("dp", "expert"), None), P("expert", "dp", None)),
        check_vma=False,
    )
```
